128 devices in a mesh: box: 32 (over x, z, core), rep: 4 (over y).
Axes of the slice: x: 4, y: 4, z: 4, core: 2. Of those that a mesh axis runs over, the one named last changes fastest.
Arguments:
- currents: bfloat16 [2, 2, 1024, 128], P(None, None, 'box'), may hold values from -6 to 6
- populations: int32 [1024], P('box'), may hold values from 1 to 128, as said below
- radiate: bfloat16 [1024, 2, 4, 64, 128], P('box', None, 'rep'), may hold values from -0.5 to 0.5
- receive: bfloat16 [1024, 2, 4, 64, 128], P('box', None, 'rep'), may hold values from -0.375 to 0.375
- translation: float32 [2, 4, 64, 316], P(None, 'rep'), may hold values from -1 to 1
- far_list: int32 [1024, 32], replicated, may hold values from 0 to 1023
- far_type: int32 [1024, 32], replicated, may hold values from 0 to 315
- near_list: int32 [1024, 8], P('box', 'rep'), may hold values from 0 to 1023, as said below
- near_block: bfloat16 [1024, 8, 2, 128, 128], P('box', 'rep'), may hold values from -0.125 to 0.125
Outputs:
- field: float32 [2, 2, 1024, 128], P(None, None, 'box')
The draws below stay inside these ranges and needn't reach their ends.
Inputs may be any that keep to these rules, and one draw needn't show every extreme that they name: `populations`: each box has at least one live slot, and some box has all 128 slots live. near_list[b, n] lies within 32 of b; near_list[b, 0] is b itself.
All inputs are finite; a program needn't handle non-finite values.
Results may differ from the reference program's by a relative error of at most 0.0026.
Values may be sent and summed in bfloat16 or wider, within the bound.
No kernel may reach another device: no remote copies, remote signals or barrier semaphores. Data moves between devices by JAX's collectives and lax.ppermute only.
A program may use at most 320 MiB of HBM per device.

```python
import jax
import jax.numpy as jnp
from jax import lax

P_SIZE = 128
BOX_DEV = 32
INC = 2
K = 256
NEAR = 8
FAR = 32
TYPES = 316
KREP = 64
BOXES = 1024
N_REP = 4


def draw_populations(key, part):
    key = jax.random.fold_in(key, 11)
    first, second = jax.random.split(key)
    counts = jax.random.randint(first, (BOXES,), 1, P_SIZE + 1)
    fullest = jax.random.randint(second, (), 0, BOXES)
    return jnp.where(jnp.arange(BOXES) == fullest, P_SIZE, counts).astype(jnp.int32)


def draw_near_list(key, part):
    key = jax.random.fold_in(key, 23)
    row = jnp.arange(BOXES)[:, None]
    column = jnp.arange(NEAR)[None, :]
    offsets = jax.random.randint(key, (BOXES, NEAR), -BOX_DEV, BOX_DEV + 1)
    below = jnp.where(row >= BOX_DEV, -BOX_DEV, BOX_DEV)
    offsets = jnp.where(column == 0, 0, offsets)
    offsets = jnp.where(column == 1, below, offsets)
    offsets = jnp.where(column == 2, BOX_DEV, offsets)
    return jnp.clip(row + offsets, 0, BOXES - 1).astype(jnp.int32)


def plant(values, rng, least, top_value):
    shape = values.shape
    place = [jax.random.randint(jax.random.fold_in(rng, axis), (), 0, shape[axis]) for axis in range(len(shape))]
    values = values.at[tuple(place)].set(least)
    longest = shape.index(max(shape))
    place[longest] = (place[longest] + 1) % shape[longest]
    return values.at[tuple(place)].set(top_value)


def block_scale(stream_key, shape, cuts, least, top_value):
    def one(dim, parts):
        draws = jax.random.uniform(jax.random.fold_in(jax.random.fold_in(stream_key, 6), dim), (parts,), jnp.float32, least / len(cuts), top_value / len(cuts))
        return jnp.repeat(jnp.exp(draws), shape[dim] // parts).reshape((-1,) + (1,) * (len(shape) - dim - 1))

    gain = one(*cuts[0])
    for cut in cuts[1:]:
        gain = gain * one(*cut)
    return gain


def normal_values(own_key, shape, deviation, most, shards=(), held_as=jnp.bfloat16):
    loudness = block_scale(own_key, shape, shards, -0.22, 0.18) if shards else 1.0
    result = jax.random.normal(own_key, shape, jnp.float32) * deviation * loudness
    return jnp.minimum(jnp.maximum(result, -most), most).astype(held_as)


def setup_inputs(seed: int = 0) -> dict:
    arg_keys = jax.random.split(jax.random.key(seed), 10)
    currents = normal_values(arg_keys[0], (2, INC, BOXES, P_SIZE), 1.0, 6.0, ((2, 32),))
    populations = draw_populations(jax.random.fold_in(arg_keys[9], 71), 0)
    radiate = normal_values(arg_keys[2], (BOXES, 2, N_REP, KREP, P_SIZE), P_SIZE ** -0.5, 0.5, ((0, 32), (2, 4)))
    receive = normal_values(arg_keys[3], (BOXES, 2, N_REP, KREP, P_SIZE), K ** -0.5, 0.375, ((0, 32), (2, 4)))
    translation = normal_values(arg_keys[4], (2, N_REP, KREP, TYPES), 0.125, 1.0, ((1, 4),), jnp.float32)
    far_list = plant(jax.random.randint(arg_keys[5], (BOXES, FAR), 0, BOXES), jax.random.fold_in(arg_keys[5], 1), 0, BOXES - 1).astype(jnp.int32)
    far_type = plant(jax.random.randint(arg_keys[6], (BOXES, FAR), 0, TYPES), jax.random.fold_in(arg_keys[6], 1), 0, TYPES - 1).astype(jnp.int32)
    near_list = draw_near_list(jax.random.fold_in(arg_keys[9], 71), 0)
    near_block = normal_values(arg_keys[8], (BOXES, NEAR, 2, P_SIZE, P_SIZE), (2 * NEAR * P_SIZE) ** -0.5, 0.125, ((0, 32), (1, 4)))
    return dict(currents=currents, populations=populations, radiate=radiate, receive=receive, translation=translation, far_list=far_list, far_type=far_type, near_list=near_list, near_block=near_block)


def complex_product(a_re, a_im, b_re, b_im, form):
    def single(a, b):
        return jnp.einsum(form, a, b)
    return single(a_re, b_re) - single(a_im, b_im), single(a_re, b_im) + single(a_im, b_re)


def reference(currents, populations, radiate, receive, translation, far_list, far_type, near_list, near_block):
    f32 = jnp.float32
    groups = BOXES // BOX_DEV
    live = jnp.arange(P_SIZE)[None, :] < populations[:, None]
    masked = jnp.where(live[None, None], currents, jnp.zeros_like(currents))
    cur_groups = jnp.moveaxis(masked.reshape(2, INC, groups, BOX_DEV, P_SIZE), 2, 0)
    rad_groups = radiate.reshape(groups, BOX_DEV, 2, K, P_SIZE)

    def aggregate(item):
        table, vec = item
        table = table.astype(f32)
        vec = vec.astype(f32)
        real, imag = complex_product(table[:, 0], table[:, 1], vec[0], vec[1], 'bkp,ibp->ikb')
        return jnp.stack([real, imag])

    pattern = jnp.moveaxis(lax.map(aggregate, (rad_groups, cur_groups)), 0, 3).reshape(2, INC, K, BOXES)
    trans = translation.reshape(2, K, TYPES)

    def far_step(f, acc):
        source = jnp.take(pattern, far_list[:, f], axis=3)
        coef = jnp.take(trans, far_type[:, f], axis=2)
        real = acc[0] + coef[0][None] * source[0] - coef[1][None] * source[1]
        imag = acc[1] + coef[0][None] * source[1] + coef[1][None] * source[0]
        return jnp.stack([real, imag])

    incoming = lax.fori_loop(0, FAR, far_step, jnp.zeros((2, INC, K, BOXES), f32)).astype(jnp.bfloat16)
    inc_groups = jnp.moveaxis(incoming.reshape(2, INC, K, groups, BOX_DEV), 3, 0)
    rcv_groups = receive.reshape(groups, BOX_DEV, 2, K, P_SIZE)
    neighbours = jnp.take(masked, near_list, axis=2)
    nb_groups = jnp.moveaxis(neighbours.reshape(2, INC, groups, BOX_DEV, NEAR, P_SIZE), 2, 0)
    blk_groups = near_block.reshape(groups, BOX_DEV, NEAR, 2, P_SIZE, P_SIZE)

    def disaggregate(item):
        table, vec, blocks, near_vec = item
        table = table.astype(f32)
        vec = vec.astype(f32)
        far_re, far_im = complex_product(table[:, 0], table[:, 1], vec[0], vec[1], 'bkp,ikb->ibp')
        blocks = blocks.astype(f32)
        near_vec = near_vec.astype(f32)
        near_re, near_im = complex_product(blocks[:, :, 0], blocks[:, :, 1], near_vec[0], near_vec[1], 'bnqp,ibnp->ibq')
        return jnp.stack([far_re + near_re, far_im + near_im])

    total = lax.map(disaggregate, (rcv_groups, inc_groups, blk_groups, nb_groups))
    total = jnp.moveaxis(total, 0, 2).reshape(2, INC, BOXES, P_SIZE)
    return jnp.where(live[None, None], total, jnp.zeros_like(total))
```

```python
import jax
import jax.numpy as jnp
from jax import lax
from jax.experimental import pallas as pl
from jax.experimental.pallas import tpu as pltpu
from jax.sharding import PartitionSpec as P

F32 = jnp.float32
BF16 = jnp.bfloat16
NT = (((1,), (1,)), ((), ()))
NN = (((1,), (0,)), ((), ()))
VMEM = pl.BlockSpec(memory_space=pltpu.VMEM)
SMEM = pl.BlockSpec(memory_space=pltpu.SMEM)
XS = ZS = 4


def iota(shape, dim):
    return lax.broadcasted_iota(jnp.int32, shape, dim)


def dot(a, b, dims=NN):
    return lax.dot_general(a, b, dims, preferred_element_type=F32)


def chip_index(x, z, core):
    return (x * ZS + z) * 2 + core


def plane_perm(move):
    places = [(x, z, c) for x in range(XS) for z in range(ZS) for c in range(2)]
    return [(chip_index(*move(*place)), chip_index(*place)) for place in places]


def from_z(d):
    return plane_perm(lambda x, z, c: (x, (z + d) % ZS, c))


def from_x(d):
    return plane_perm(lambda x, z, c: ((x + d) % XS, z, c))


def from_core():
    return plane_perm(lambda x, z, c: (x, z, 1 - c))


def from_next_chip():
    def move(x, z, c):
        chip = (x * ZS + z + (1 if c else -1)) % (XS * ZS)
        return chip // ZS, chip % ZS, 1 - c

    return plane_perm(move)


def live_rows(pop_ref, boxes, slots):
    row = iota((boxes, slots), 0)
    count = jnp.zeros((boxes, slots), jnp.int32)
    for b in range(boxes):
        count = jnp.where(row == b, pop_ref[b], count)
    return iota((boxes, slots), 1) < count


def pattern_kernel(pop_ref, cur_ref, rad_ref, masked_ref, pat_ref):
    lines, boxes, slots = cur_ref.shape
    live = live_rows(pop_ref, boxes, slots)
    masked = [jnp.where(live, cur_ref[j].astype(F32), 0.0) for j in range(lines)]
    for j in range(lines):
        masked_ref[j] = masked[j].astype(BF16)
    rows = jnp.concatenate(masked, axis=0)
    box_of_row = iota(rows.shape, 0) & (boxes - 1)
    total = jnp.zeros((lines * boxes, slots), F32)
    for b in range(0, boxes, 2):
        left = jnp.concatenate(
            [jnp.where(box_of_row == b + h, rows, 0.0).astype(BF16) for h in range(2)], axis=1
        )
        right = jnp.concatenate([rad_ref[b], rad_ref[b + 1]], axis=1)
        total = total + dot(left, right, NT)
    half = slots // 2
    sign = jnp.where(iota((boxes, slots), 1) < half, -1.0, 1.0)
    for i in range(2):
        real = total[i * boxes : (i + 1) * boxes]
        imag = total[(2 + i) * boxes : (3 + i) * boxes]
        out = real + sign * pltpu.roll(imag, half, 1)
        pat_ref[:, i * slots : (i + 1) * slots] = out.astype(BF16)


def coef_kernel(type_ref, trans_ref, coef_ref, table_ref):
    boxes, far = type_ref.shape
    half, types = trans_ref.shape[1:]
    wide = table_ref.shape[2]
    table_ref[...] = jnp.zeros_like(table_ref)
    for c in range(2):
        value = trans_ref[c]
        high = value.astype(BF16)
        low = (value - high.astype(F32)).astype(BF16)
        for k in range(2):
            place = pl.ds((2 * c + k) * half, half)
            table_ref[0, place, :types] = high
            table_ref[1, place, :types] = low
    lane = iota((boxes, wide), 1)
    pieces = []
    for f in range(far):
        column = type_ref[:, f : f + 1]
        pieces.append(jnp.where(lane == column, 1.0, 0.0).astype(BF16))
    hot = jnp.concatenate(pieces, axis=0)
    coef_ref[...] = dot(hot, table_ref[0], NT) + dot(hot, table_ref[1], NT)


def near_kernel(pop_ref, list_ref, own_ref, core_ref, next_ref, block_ref, out_ref):
    lines, boxes, slots = own_ref.shape
    pairs = list_ref.shape[1]
    place = lax.axis_index("box")
    core = place & 1
    beyond = place + 2 * core - 1
    lane = iota((boxes, slots), 1)
    first = jnp.where(
        lane < boxes,
        place * boxes,
        jnp.where(lane < 2 * boxes, (place + 1 - 2 * core) * boxes, beyond * boxes),
    )
    ids = jnp.where(lane < 3 * boxes, first + (lane & (boxes - 1)), -1000000)
    hot = jnp.concatenate(
        [jnp.where(ids == list_ref[:, n : n + 1], 1.0, 0.0).astype(BF16) for n in range(pairs)],
        axis=0,
    )
    zero = jnp.zeros((slots - 3 * boxes, slots), BF16)
    picked = []
    for j in range(lines):
        source = jnp.concatenate([own_ref[j], core_ref[j], next_ref[j], zero], axis=0)
        picked.append(dot(hot, source))
    box_of_row = iota((lines * boxes, slots), 0) & (boxes - 1)
    lefts = []
    for n in range(pairs):
        part = [value[n * boxes : (n + 1) * boxes] for value in picked]
        lefts.append(jnp.concatenate(part, axis=0))
        lefts.append(jnp.concatenate([-part[2], -part[3], part[0], part[1]], axis=0))
    total = jnp.zeros((lines * boxes, slots), F32)
    for b in range(boxes):
        mine = box_of_row == b
        for n in range(pairs):
            left = jnp.concatenate(
                [jnp.where(mine, lefts[2 * n + c], 0.0).astype(BF16) for c in range(2)], axis=1
            )
            right = jnp.concatenate([block_ref[b, n, 0], block_ref[b, n, 1]], axis=1)
            total = total + dot(left, right, NT)
    out_ref[...] = total


def far_kernel(
    pop_ref, list_ref, coef_ref, near_ref, mine_ref, theirs_ref, receive_ref, out_ref
):
    boxes, far = list_ref.shape
    slots = receive_ref.shape[2]
    held, wide = mine_ref.shape
    place = lax.axis_index("box")
    core = place & 1
    chip = place >> 1
    x, z = chip >> 2, chip & 3
    lane = iota((boxes, held), 1)
    from_x_ = (x + (lane >> 7)) & 3
    from_z_ = (z + ((lane >> 5) & 3)) & 3
    ids = (((from_x_ * ZS + from_z_) * 2 + core) * boxes) + (lane & (boxes - 1))
    other = ids + (1 - 2 * core) * boxes
    acc = [jnp.zeros((boxes, slots), F32) for _ in range(4)]
    group = 8
    for f in range(0, far, group):
        columns = [list_ref[:, g : g + 1] for g in range(f, f + group)]
        hot_mine = jnp.concatenate(
            [jnp.where(ids == col, 1.0, 0.0).astype(BF16) for col in columns], axis=0
        )
        hot_theirs = jnp.concatenate(
            [jnp.where(other == col, 1.0, 0.0).astype(BF16) for col in columns], axis=0
        )
        source = dot(hot_mine, mine_ref[...]) + dot(hot_theirs, theirs_ref[...])
        for g in range(group):
            rows = slice(g * boxes, (g + 1) * boxes)
            at = (f + g) * boxes
            straight = coef_ref[at : at + boxes, :slots]
            crossed = coef_ref[at : at + boxes, slots:]
            for i in range(2):
                value = source[rows, i * slots : (i + 1) * slots]
                acc[2 * i] = acc[2 * i] + straight * value
                acc[2 * i + 1] = acc[2 * i + 1] + crossed * value
    half = slots // 2
    low = iota((boxes, slots), 1) < half
    minus = jnp.where(low, -1.0, 1.0)
    reals, imags = [], []
    for i in range(2):
        incoming = acc[2 * i] + minus * pltpu.roll(acc[2 * i + 1], half, 1)
        incoming = incoming.astype(BF16).astype(F32)
        reals.append(-minus * incoming)
        imags.append(pltpu.roll(incoming, half, 1))
    left_rows = jnp.concatenate(reals + imags, axis=0)
    box_of_row = iota(left_rows.shape, 0) & (boxes - 1)
    total = near_ref[...]
    for b in range(0, boxes, 2):
        left = jnp.concatenate(
            [jnp.where(box_of_row == b + h, left_rows, 0.0).astype(BF16) for h in range(2)], axis=1
        )
        right = jnp.concatenate([receive_ref[b], receive_ref[b + 1]], axis=0)
        total = total + dot(left, right)
    live = live_rows(pop_ref, boxes, slots)
    for j in range(4):
        out_ref[j] = jnp.where(live, total[j * boxes : (j + 1) * boxes], 0.0)


def call(kernel, out_shape, specs, out_specs, scratch=(), flops=0, size=0):
    return pl.pallas_call(
        kernel,
        out_shape=out_shape,
        in_specs=specs,
        out_specs=out_specs,
        scratch_shapes=list(scratch),
        cost_estimate=pl.CostEstimate(flops=flops, bytes_accessed=size, transcendentals=0),
        compiler_params=pltpu.CompilerParams(vmem_limit_bytes=32 * 1024 * 1024),
    )


def body(
    currents, populations, radiate, receive, translation, far_list, far_type, near_list, near_block
):
    place = lax.axis_index("box")
    incs, boxes, slots = currents.shape[1:]
    lines = 2 * incs
    half = radiate.shape[3]
    far = far_list.shape[1]
    shape = jax.ShapeDtypeStruct
    cur = currents.reshape(lines, boxes, slots)
    rad = radiate.reshape(boxes, 2 * half, slots)
    rec = receive.reshape(boxes, 2 * half, slots)
    trans = translation.reshape(2, half, translation.shape[3])
    block = near_block
    own_list = lax.dynamic_slice_in_dim(far_list, place * boxes, boxes, 0)
    own_type = lax.dynamic_slice_in_dim(far_type, place * boxes, boxes, 0)

    masked, pattern = call(
        pattern_kernel,
        (shape((lines, boxes, slots), BF16), shape((boxes, incs * slots), BF16)),
        [SMEM, VMEM, VMEM],
        (VMEM, VMEM),
    )(populations, cur, rad)

    around = [lax.ppermute(pattern, "box", from_z(d)) for d in (1, 2, 3)]
    line = jnp.concatenate([pattern] + around, axis=0)
    planes = [lax.ppermute(line, "box", from_x(d)) for d in (1, 2, 3)]
    mine = jnp.concatenate([line] + planes, axis=0)
    theirs = lax.ppermute(mine, "box", from_core())

    near_core = lax.ppermute(masked, "box", from_core())
    near_next = lax.ppermute(masked, "box", from_next_chip())

    types = trans.shape[2]
    padded = -(-types // 128) * 128
    coef = call(
        coef_kernel,
        shape((far * boxes, 2 * slots), F32),
        [VMEM, VMEM],
        VMEM,
        [pltpu.VMEM((2, 4 * half, padded), BF16)],
    )(own_type, trans)

    near = call(
        near_kernel,
        shape((lines * boxes, slots), F32),
        [SMEM, VMEM, VMEM, VMEM, VMEM, VMEM],
        VMEM,
    )(populations, near_list, masked, near_core, near_next, block)

    part = call(
        far_kernel,
        shape((lines, boxes, slots), F32),
        [SMEM] + [VMEM] * 6,
        VMEM,
    )(populations, own_list, coef, near, mine, theirs, rec)

    reps = lax.axis_size("rep")
    others = [
        lax.ppermute(part, "rep", [((r + d) % reps, r) for r in range(reps)]) for d in (1, 2, 3)
    ]
    total = (part + others[1]) + (others[0] + others[2])
    return total.reshape(2, incs, boxes, slots)


def solution(mesh):
    return jax.shard_map(
        body,
        mesh=mesh,
        in_specs=(
            P(None, None, "box", None),
            P("box"),
            P("box", None, "rep", None, None),
            P("box", None, "rep", None, None),
            P(None, "rep", None, None),
            P(),
            P(),
            P("box", "rep"),
            P("box", "rep", None, None, None),
        ),
        out_specs=P(None, None, "box", None),
        check_vma=False,
    )
```

```python
import jax
import jax.numpy as jnp
from jax import lax
from jax.experimental import pallas as pl
from jax.experimental.pallas import tpu as pltpu
from jax.sharding import PartitionSpec as P

F32 = jnp.float32
BF16 = jnp.bfloat16
NT = (((1,), (1,)), ((), ()))
NN = (((1,), (0,)), ((), ()))
VMEM = pl.BlockSpec(memory_space=pltpu.VMEM)
HBM = pl.BlockSpec(memory_space=pltpu.HBM)
XS = ZS = 4


def iota(shape, dim):
    return lax.broadcasted_iota(jnp.int32, shape, dim)


def dot(a, b, dims=NN):
    return lax.dot_general(a, b, dims, preferred_element_type=F32)


LINES = (
    ((0, False, False), (-1, False, True), (1, False, True), (2, True, False)),
    ((0, False, False), (1, False, True), (-1, False, True), (2, True, False)),
)
PLANES = (2, 3, 1)
REPS = (1, 3, 2)


def moved(chip, move, along_z):
    if along_z:
        return chip // ZS * ZS + (chip + move) % ZS
    return (chip + move) % (XS * ZS)


def box_perm(source):
    places = [(chip, core) for chip in range(XS * ZS) for core in range(2)]
    pairs = []
    for chip, core in places:
        from_chip, from_core = source(chip, core)
        pairs.append((from_chip * 2 + from_core, chip * 2 + core))
    return pairs


def from_line(step):
    def source(chip, core):
        move, along_z, cross = LINES[core][step]
        return moved(chip, move, along_z), 1 - core if cross else core

    return box_perm(source)


def from_plane(d):
    return box_perm(lambda chip, core: (moved(chip, d * ZS, False), core))


def from_core():
    return box_perm(lambda chip, core: (chip, 1 - core))


def column(row):
    boxes = row.shape[1]
    diagonal = iota((boxes, boxes), 0) == iota((boxes, boxes), 1)
    return jnp.sum(jnp.where(diagonal, row, 0).astype(F32), axis=1, keepdims=True).astype(jnp.int32)


def own_columns(tile, boxes):
    place = lax.axis_index("box")
    start = (place & (128 // boxes - 1)) * boxes
    moved = pltpu.roll(tile, lax.rem(128 - start, 128), 1)
    return jnp.transpose(moved.astype(F32))[:boxes].astype(jnp.int32)


def live_rows(pop_ref, boxes, slots):
    return iota((boxes, slots), 1) < column(pop_ref[...])


def pattern_kernel(
    pop_hbm, cur_hbm, rad_hbm, list_hbm, type_hbm, near_hbm, trans_hbm,
    pay_ref, pat_ref, masked_ref, pop_ref, list_ref, type_ref, near_ref, trans_ref,
    cur_ref, rad_ref, sems,
):
    lines, boxes, slots = cur_ref.shape
    place = lax.axis_index("box")
    tile = pl.multiple_of((place >> 2) * 128, 128)
    copies = [
        pltpu.make_async_copy(pop_hbm, pop_ref, sems.at[0]),
        pltpu.make_async_copy(cur_hbm, cur_ref, sems.at[1]),
        pltpu.make_async_copy(rad_hbm, rad_ref, sems.at[2]),
        pltpu.make_async_copy(list_hbm.at[:, pl.ds(tile, 128)], list_ref, sems.at[3]),
        pltpu.make_async_copy(type_hbm.at[:, pl.ds(tile, 128)], type_ref, sems.at[4]),
        pltpu.make_async_copy(near_hbm, near_ref, sems.at[5]),
        pltpu.make_async_copy(trans_hbm, trans_ref, sems.at[6]),
    ]
    for copy in copies:
        copy.start()
    copies[0].wait()
    live = live_rows(pop_ref, boxes, slots)
    copies[1].wait()
    masked = [jnp.where(live, cur_ref[j].astype(F32), 0.0) for j in range(lines)]
    for j in range(lines):
        pay_ref[:, (2 + j) * slots : (3 + j) * slots] = masked[j].astype(BF16)
        masked_ref[:, j * slots : (j + 1) * slots] = masked[j].astype(BF16)
    rows = jnp.concatenate(masked, axis=0)
    box_of_row = iota(rows.shape, 0) & (boxes - 1)
    copies[2].wait()
    total = jnp.zeros((lines * boxes, slots), F32)
    for b in range(0, boxes, 2):
        left = jnp.concatenate(
            [jnp.where(box_of_row == b + h, rows, 0.0).astype(BF16) for h in range(2)], axis=1
        )
        right = jnp.concatenate([rad_ref[b], rad_ref[b + 1]], axis=1)
        total = total + dot(left, right, NT)
    half = slots // 2
    sign = jnp.where(iota((boxes, slots), 1) < half, -1.0, 1.0)
    for i in range(2):
        real = total[i * boxes : (i + 1) * boxes]
        imag = total[(2 + i) * boxes : (3 + i) * boxes]
        out = real + sign * pltpu.roll(imag, half, 1)
        pay_ref[:, i * slots : (i + 1) * slots] = out.astype(BF16)
        pat_ref[:, i * slots : (i + 1) * slots] = out.astype(BF16)
    for copy in copies[3:]:
        copy.wait()


def coef_kernel(
    type_ref, trans_ref, pat_ref, block_hbm, coef_ref, pass_ref, block_ref, table_ref, sem
):
    fetch = pltpu.make_async_copy(block_hbm, block_ref, sem)
    fetch.start()
    far = type_ref.shape[0]
    boxes = pat_ref.shape[0]
    half, types = trans_ref.shape[1:]
    wide = table_ref.shape[2]
    pass_ref[...] = pat_ref[...]
    table_ref[...] = jnp.zeros_like(table_ref)
    for c in range(2):
        value = trans_ref[c]
        high = value.astype(BF16)
        low = (value - high.astype(F32)).astype(BF16)
        for k in range(2):
            place = pl.ds((2 * c + k) * half, half)
            table_ref[0, place, :types] = high
            table_ref[1, place, :types] = low
    lane = iota((boxes, wide), 1)
    kinds = own_columns(type_ref[...], boxes)
    pieces = []
    for f in range(far):
        pieces.append(jnp.where(lane == kinds[:, f : f + 1], 1.0, 0.0).astype(BF16))
    hot = jnp.concatenate(pieces, axis=0)
    coef_ref[...] = dot(hot, table_ref[0], NT) + dot(hot, table_ref[1], NT)
    fetch.wait()


def box_ids(boxes, theirs):
    place = lax.axis_index("box")
    core, chip = place & 1, place >> 1
    holder = 1 - core if theirs else core
    lane = iota((1, XS * ZS * boxes), 1)
    plane = lane // (ZS * boxes)
    slot = (lane // boxes) & (ZS - 1)
    first = jnp.full(lane.shape, 0, jnp.int32)
    for step in range(ZS):
        at = []
        for move, along_z, _ in (LINES[0][step], LINES[1][step]):
            at.append((chip & ~3) + ((chip + move) & 3) if along_z else (chip + move) & 15)
        first = jnp.where(slot == step, jnp.where(holder == 0, at[0], at[1]), first)
    shift = jnp.zeros_like(lane)
    for j, d in enumerate(PLANES):
        shift = jnp.where(plane == j + 1, d * ZS, shift)
    cross = jnp.where((slot == 1) | (slot == 2), 1, 0)
    return ((((first + shift) & 15) * 2 + (holder ^ cross)) * boxes) + (lane & (boxes - 1))


def translate(listed, ids, coef_ref, source_ref, acc):
    boxes, far = listed.shape
    slots = coef_ref.shape[1] // 2
    group = 8
    for f in range(0, far, group):
        hot = jnp.concatenate(
            [
                jnp.where(ids == listed[:, g : g + 1], 1.0, 0.0).astype(BF16)
                for g in range(f, f + group)
            ],
            axis=0,
        )
        source = dot(hot, source_ref[...])
        for g in range(group):
            rows = slice(g * boxes, (g + 1) * boxes)
            at = (f + g) * boxes
            straight = coef_ref[at : at + boxes, :slots]
            crossed = coef_ref[at : at + boxes, slots:]
            for i in range(2):
                value = source[rows, i * slots : (i + 1) * slots]
                acc[2 * i] = acc[2 * i] + straight * value
                acc[2 * i + 1] = acc[2 * i + 1] + crossed * value
    return acc


def near_kernel(
    list_ref, own_ref, core_ref, next_ref, held_ref, block_ref, out_ref, pass_ref
):
    pairs, boxes = list_ref.shape
    slots = out_ref.shape[1]
    lines = own_ref.shape[1] // slots
    pass_ref[...] = held_ref[...]
    place = lax.axis_index("box")
    core = place & 1
    beyond = place + 2 * core - 1
    lane = iota((boxes, slots), 1)
    first = jnp.where(
        lane < boxes,
        place * boxes,
        jnp.where(lane < 2 * boxes, (place + 1 - 2 * core) * boxes, beyond * boxes),
    )
    ids = jnp.where(lane < 3 * boxes, first + (lane & (boxes - 1)), -1000000)
    hot = jnp.concatenate(
        [
            jnp.where(ids == column(list_ref[n : n + 1, :]), 1.0, 0.0).astype(BF16)
            for n in range(pairs)
        ],
        axis=0,
    )
    zero = jnp.zeros((slots - 3 * boxes, lines * slots), BF16)
    source = jnp.concatenate([own_ref[...], core_ref[...], next_ref[...], zero], axis=0)
    found = dot(hot, source)
    picked = [found[:, j * slots : (j + 1) * slots] for j in range(lines)]
    box_of_row = iota((lines * boxes, slots), 0) & (boxes - 1)
    lefts = []
    for n in range(pairs):
        part = [value[n * boxes : (n + 1) * boxes] for value in picked]
        lefts.append(jnp.concatenate(part, axis=0))
        lefts.append(jnp.concatenate([-part[2], -part[3], part[0], part[1]], axis=0))
    total = jnp.zeros((lines * boxes, slots), F32)
    for b in range(boxes):
        mine = box_of_row == b
        for n in range(pairs):
            left = jnp.concatenate(
                [jnp.where(mine, lefts[2 * n + c], 0.0).astype(BF16) for c in range(2)], axis=1
            )
            right = jnp.concatenate([block_ref[b, n, 0], block_ref[b, n, 1]], axis=1)
            total = total + dot(left, right, NT)
    out_ref[...] = total


def mine_kernel(list_ref, coef_ref, mine_ref, acc_ref):
    boxes, slots = acc_ref.shape[1:]
    listed = own_columns(list_ref[...], boxes)
    ids = box_ids(boxes, False)
    acc = [jnp.zeros((boxes, slots), F32) for _ in range(4)]
    acc = translate(listed, ids, coef_ref, mine_ref, acc)
    for j in range(4):
        acc_ref[j] = acc[j]


def far_kernel(
    pop_ref, list_ref, coef_ref, near_ref, acc_ref, theirs_ref, receive_ref, out_ref
):
    boxes, slots = receive_ref.shape[0], receive_ref.shape[2]
    listed = own_columns(list_ref[...], boxes)
    ids = box_ids(boxes, True)
    acc = translate(listed, ids, coef_ref, theirs_ref, [acc_ref[j] for j in range(4)])
    half = slots // 2
    low = iota((boxes, slots), 1) < half
    minus = jnp.where(low, -1.0, 1.0)
    reals, imags = [], []
    for i in range(2):
        incoming = acc[2 * i] + minus * pltpu.roll(acc[2 * i + 1], half, 1)
        reals.append(-minus * incoming)
        imags.append(pltpu.roll(incoming, half, 1))
    exact = jnp.concatenate(reals + imags, axis=0)
    high = exact.astype(BF16).astype(F32)
    left_rows = jnp.concatenate([high, exact - high], axis=0)
    box_of_row = iota(left_rows.shape, 0) & (boxes - 1)
    total = jnp.zeros(left_rows.shape, F32)
    for b in range(0, boxes, 2):
        left = jnp.concatenate(
            [jnp.where(box_of_row == b + h, left_rows, 0.0).astype(BF16) for h in range(2)], axis=1
        )
        right = jnp.concatenate([receive_ref[b], receive_ref[b + 1]], axis=0)
        total = total + dot(left, right)
    total = (total[: 4 * boxes] + total[4 * boxes :]) + near_ref[...]
    live = live_rows(pop_ref, boxes, slots)
    for j in range(4):
        out_ref[j] = jnp.where(live, total[j * boxes : (j + 1) * boxes], 0.0)


def call(kernel, out_shape, specs, out_specs, scratch=(), flops=0, size=0):
    return pl.pallas_call(
        kernel,
        out_shape=out_shape,
        in_specs=specs,
        out_specs=out_specs,
        scratch_shapes=list(scratch),
        cost_estimate=pl.CostEstimate(flops=flops, bytes_accessed=size, transcendentals=0),
        compiler_params=pltpu.CompilerParams(vmem_limit_bytes=32 * 1024 * 1024),
    )


def stay(array):
    return pltpu.with_memory_space_constraint(array, pltpu.HBM)


def body(
    currents, populations, radiate, receive, translation, far_list, far_type, near_list, near_block
):
    incs, boxes, slots = currents.shape[1:]
    lines = 2 * incs
    half = radiate.shape[3]
    far = far_list.shape[1]
    types = translation.shape[3]
    pairs = near_list.shape[1]
    wide = incs * slots
    shape = jax.ShapeDtypeStruct

    payload, pattern, masked, pop, listed, kinds, partners, trans = call(
        pattern_kernel,
        (
            shape((boxes, wide + lines * slots), BF16),
            shape((boxes, wide), BF16),
            shape((boxes, lines * slots), BF16),
            shape((1, boxes), jnp.int32),
            shape((far, 128), jnp.int32),
            shape((far, 128), jnp.int32),
            shape((pairs, boxes), jnp.int32),
            shape((2, half, types), F32),
        ),
        [HBM] * 7,
        (VMEM,) * 8,
        [
            pltpu.VMEM((lines, boxes, slots), BF16),
            pltpu.VMEM((boxes, 2 * half, slots), BF16),
            pltpu.SemaphoreType.DMA((7,)),
        ],
        flops=2 * 128 * 4096 * 128,
        size=1 << 20,
    )(
        stay(populations.reshape(1, boxes)),
        stay(currents.reshape(lines, boxes, slots)),
        stay(radiate.reshape(boxes, 2 * half, slots)),
        stay(far_list.T),
        stay(far_type.T),
        stay(near_list.T),
        stay(translation.reshape(2, half, types)),
    )

    third = lax.ppermute(pattern, "box", from_line(2))
    second = lax.ppermute(payload, "box", from_line(1))
    fourth = lax.ppermute(pattern, "box", from_line(3))
    near_core = lax.ppermute(masked, "box", from_core())

    padded = -(-types // 128) * 128
    coef, pattern, block = call(
        coef_kernel,
        (
            shape((far * boxes, 2 * slots), F32),
            shape(pattern.shape, BF16),
            pltpu.VMEM(near_block.shape, BF16),
        ),
        [VMEM] * 3 + [HBM],
        (VMEM,) * 3,
        [pltpu.VMEM((2, 4 * half, padded), BF16), pltpu.SemaphoreType.DMA(())],
        flops=4 * far * boxes * padded * 2 * slots,
        size=4 << 20,
    )(kinds, trans, pattern, stay(near_block))

    held = jnp.concatenate([pattern, second[:, :wide], third, fourth], axis=0)
    planes = [lax.ppermute(held, "box", from_plane(d)) for d in PLANES]

    near, held = call(
        near_kernel,
        (shape((lines * boxes, slots), F32), shape(held.shape, BF16)),
        [VMEM] * 6,
        (VMEM, VMEM),
        flops=2 * 128 * near_block.size // 128 * 128,
        size=near_block.size,
    )(partners, masked, near_core, second[:, wide:], held, block)

    mine = jnp.concatenate([held] + planes, axis=0)
    theirs = lax.ppermute(mine, "box", from_core())
    acc = call(
        mine_kernel,
        shape((lines, boxes, slots), F32),
        [VMEM] * 3,
        VMEM,
        flops=1024 * 1024 * 256,
        size=2 << 20,
    )(listed, coef, mine)

    part = call(
        far_kernel,
        shape((lines, boxes, slots), F32),
        [VMEM] * 7,
        VMEM,
        flops=1024 * 1024 * 256,
        size=4 << 20,
    )(pop, listed, coef, near, acc, theirs, receive.reshape(boxes, 2 * half, slots))

    reps = lax.axis_size("rep")
    others = {
        d: lax.ppermute(part, "rep", [(r ^ d, r) for r in range(reps)]) for d in REPS
    }
    total = (part + others[1]) + (others[2] + others[3])
    return total.reshape(2, incs, boxes, slots)


def solution(mesh):
    return jax.shard_map(
        body,
        mesh=mesh,
        in_specs=(
            P(None, None, "box", None),
            P("box"),
            P("box", None, "rep", None, None),
            P("box", None, "rep", None, None),
            P(None, "rep", None, None),
            P(),
            P(),
            P("box", "rep"),
            P("box", "rep", None, None, None),
        ),
        out_specs=P(None, None, "box", None),
        check_vma=False,
    )
```

```python
import jax
import jax.numpy as jnp
from jax import lax
from jax.experimental import pallas as pl
from jax.experimental.pallas import tpu as pltpu
from jax.sharding import PartitionSpec as P

F32 = jnp.float32
BF16 = jnp.bfloat16
NT = (((1,), (1,)), ((), ()))
NN = (((1,), (0,)), ((), ()))
VMEM = pl.BlockSpec(memory_space=pltpu.VMEM)
HBM = pl.BlockSpec(memory_space=pltpu.HBM)
XS = ZS = 4


def iota(shape, dim):
    return lax.broadcasted_iota(jnp.int32, shape, dim)


def dot(a, b, dims=NN):
    return lax.dot_general(a, b, dims, preferred_element_type=F32)


MOVES = {
    "own": ((0, False, False), (0, False, False)),
    "next": ((-1, False, True), (1, False, True)),
    "back": ((1, False, True), (-1, False, True)),
    "across": ((2, True, False), (2, True, False)),
}
ORDER = ("own", "next", "across", "back")
LINES = tuple(tuple(MOVES[name][core] for name in ORDER) for core in range(2))
PLANES = (2, 3, 1)
REPS = (1, 3, 2)


def moved(chip, move, along_z):
    if along_z:
        return chip // ZS * ZS + (chip + move) % ZS
    return (chip + move) % (XS * ZS)


def box_perm(source):
    places = [(chip, core) for chip in range(XS * ZS) for core in range(2)]
    pairs = []
    for chip, core in places:
        from_chip, from_core = source(chip, core)
        pairs.append((from_chip * 2 + from_core, chip * 2 + core))
    return pairs


def from_line(step):
    def source(chip, core):
        move, along_z, cross = LINES[core][step]
        return moved(chip, move, along_z), 1 - core if cross else core

    return box_perm(source)


def from_plane(d):
    return box_perm(lambda chip, core: (moved(chip, d * ZS, False), core))


def from_core():
    return box_perm(lambda chip, core: (chip, 1 - core))


def column(row):
    boxes = row.shape[1]
    diagonal = iota((boxes, boxes), 0) == iota((boxes, boxes), 1)
    return jnp.sum(jnp.where(diagonal, row, 0).astype(F32), axis=1, keepdims=True).astype(jnp.int32)


def own_columns(tile, boxes):
    place = lax.axis_index("box")
    start = (place & (128 // boxes - 1)) * boxes
    moved = pltpu.roll(tile, lax.rem(128 - start, 128), 1)
    return jnp.transpose(moved.astype(F32))[:boxes].astype(jnp.int32)


def live_rows(pop_ref, boxes, slots):
    return iota((boxes, slots), 1) < column(pop_ref[...])


def pattern_kernel(
    pop_hbm, cur_hbm, rad_hbm, list_hbm, type_hbm, near_hbm, trans_hbm,
    pay_ref, pat_ref, masked_ref, pop_ref, list_ref, type_ref, near_ref, trans_ref,
    cur_ref, rad_ref, sems,
):
    lines, boxes, slots = cur_ref.shape
    place = lax.axis_index("box")
    tile = pl.multiple_of((place >> 2) * 128, 128)
    copies = [
        pltpu.make_async_copy(pop_hbm, pop_ref, sems.at[0]),
        pltpu.make_async_copy(cur_hbm, cur_ref, sems.at[1]),
        pltpu.make_async_copy(rad_hbm, rad_ref, sems.at[2]),
        pltpu.make_async_copy(list_hbm.at[:, pl.ds(tile, 128)], list_ref, sems.at[3]),
        pltpu.make_async_copy(type_hbm.at[:, pl.ds(tile, 128)], type_ref, sems.at[4]),
        pltpu.make_async_copy(near_hbm, near_ref, sems.at[5]),
        pltpu.make_async_copy(trans_hbm, trans_ref, sems.at[6]),
    ]
    for copy in copies:
        copy.start()
    copies[0].wait()
    live = live_rows(pop_ref, boxes, slots)
    copies[1].wait()
    masked = [jnp.where(live, cur_ref[j].astype(F32), 0.0) for j in range(lines)]
    for j in range(lines):
        pay_ref[:, (2 + j) * slots : (3 + j) * slots] = masked[j].astype(BF16)
        masked_ref[:, j * slots : (j + 1) * slots] = masked[j].astype(BF16)
    rows = jnp.concatenate(masked, axis=0)
    box_of_row = iota(rows.shape, 0) & (boxes - 1)
    copies[2].wait()
    total = jnp.zeros((lines * boxes, slots), F32)
    for b in range(0, boxes, 2):
        left = jnp.concatenate(
            [jnp.where(box_of_row == b + h, rows, 0.0).astype(BF16) for h in range(2)], axis=1
        )
        right = jnp.concatenate([rad_ref[b], rad_ref[b + 1]], axis=1)
        total = total + dot(left, right, NT)
    half = slots // 2
    sign = jnp.where(iota((boxes, slots), 1) < half, -1.0, 1.0)
    for i in range(2):
        real = total[i * boxes : (i + 1) * boxes]
        imag = total[(2 + i) * boxes : (3 + i) * boxes]
        out = real + sign * pltpu.roll(imag, half, 1)
        pay_ref[:, i * slots : (i + 1) * slots] = out.astype(BF16)
        pat_ref[:, i * slots : (i + 1) * slots] = out.astype(BF16)
    for copy in copies[3:]:
        copy.wait()


def coef_kernel(
    type_ref, trans_ref, pat_ref, block_hbm, coef_ref, pass_ref, block_ref, table_ref, sem
):
    fetch = pltpu.make_async_copy(block_hbm.at[pl.ds(0, block_ref.shape[0])], block_ref, sem)
    fetch.start()
    far = type_ref.shape[0]
    boxes = pat_ref.shape[0]
    half, types = trans_ref.shape[1:]
    wide = table_ref.shape[2]
    pass_ref[...] = pat_ref[...]
    table_ref[...] = jnp.zeros_like(table_ref)
    for c in range(2):
        value = trans_ref[c]
        high = value.astype(BF16)
        low = (value - high.astype(F32)).astype(BF16)
        for k in range(2):
            place = pl.ds((2 * c + k) * half, half)
            table_ref[0, place, :types] = high
            table_ref[1, place, :types] = low
    lane = iota((boxes, wide), 1)
    kinds = own_columns(type_ref[...], boxes)
    pieces = []
    for f in range(far):
        pieces.append(jnp.where(lane == kinds[:, f : f + 1], 1.0, 0.0).astype(BF16))
    hot = jnp.concatenate(pieces, axis=0)
    coef_ref[...] = dot(hot, table_ref[0], NT) + dot(hot, table_ref[1], NT)
    fetch.wait()


def box_ids(boxes, theirs):
    place = lax.axis_index("box")
    core, chip = place & 1, place >> 1
    holder = 1 - core if theirs else core
    lane = iota((1, XS * ZS * boxes), 1)
    plane = lane // (ZS * boxes)
    slot = (lane // boxes) & (ZS - 1)
    first = jnp.full(lane.shape, 0, jnp.int32)
    for step in range(ZS):
        at = []
        for move, along_z, _ in (LINES[0][step], LINES[1][step]):
            at.append((chip & ~3) + ((chip + move) & 3) if along_z else (chip + move) & 15)
        first = jnp.where(slot == step, jnp.where(holder == 0, at[0], at[1]), first)
    shift = jnp.zeros_like(lane)
    for j, d in enumerate(PLANES):
        shift = jnp.where(plane == j + 1, d * ZS, shift)
    cross = jnp.zeros_like(lane)
    for step in range(ZS):
        if LINES[0][step][2]:
            cross = jnp.where(slot == step, 1, cross)
    return ((((first + shift) & 15) * 2 + (holder ^ cross)) * boxes) + (lane & (boxes - 1))


def translate(listed, ids, coef_ref, source_ref, acc):
    boxes, far = listed.shape
    slots = coef_ref.shape[1] // 2
    group = 8
    for f in range(0, far, group):
        hot = jnp.concatenate(
            [
                jnp.where(ids == listed[:, g : g + 1], 1.0, 0.0).astype(BF16)
                for g in range(f, f + group)
            ],
            axis=0,
        )
        source = dot(hot, source_ref[...])
        for g in range(group):
            rows = slice(g * boxes, (g + 1) * boxes)
            at = (f + g) * boxes
            straight = coef_ref[at : at + boxes, :slots]
            crossed = coef_ref[at : at + boxes, slots:]
            for i in range(2):
                value = source[rows, i * slots : (i + 1) * slots]
                acc[2 * i] = acc[2 * i] + straight * value
                acc[2 * i + 1] = acc[2 * i + 1] + crossed * value
    return acc


def add_near(total, found, block_ref, start):
    lines, pairs = 4, block_ref.shape[1]
    boxes, slots = found.shape[0] // pairs, found.shape[1] // lines
    box_of_row = iota((lines * boxes, slots), 0) & (boxes - 1)
    lefts = []
    for n in range(pairs):
        part = [
            found[n * boxes : (n + 1) * boxes, j * slots : (j + 1) * slots] for j in range(lines)
        ]
        lefts.append(jnp.concatenate(part, axis=0))
        lefts.append(jnp.concatenate([-part[2], -part[3], part[0], part[1]], axis=0))
    for b in range(block_ref.shape[0]):
        mine = box_of_row == start + b
        for n in range(pairs):
            left = jnp.concatenate(
                [jnp.where(mine, lefts[2 * n + c], 0.0).astype(BF16) for c in range(2)], axis=1
            )
            right = jnp.concatenate([block_ref[b, n, 0], block_ref[b, n, 1]], axis=1)
            total = total + dot(left, right, NT)
    return total


def near_kernel(
    list_ref, own_ref, core_ref, next_ref, held_ref, block_ref, block_hbm,
    out_ref, found_ref, pass_ref, rest_ref, sem,
):
    start = block_ref.shape[0]
    fetch = pltpu.make_async_copy(block_hbm.at[pl.ds(start, rest_ref.shape[0])], rest_ref, sem)
    fetch.start()
    pairs, boxes = list_ref.shape
    slots = out_ref.shape[1]
    lines = own_ref.shape[1] // slots
    pass_ref[...] = held_ref[...]
    place = lax.axis_index("box")
    core = place & 1
    beyond = place + 2 * core - 1
    lane = iota((boxes, slots), 1)
    first = jnp.where(
        lane < boxes,
        place * boxes,
        jnp.where(lane < 2 * boxes, (place + 1 - 2 * core) * boxes, beyond * boxes),
    )
    ids = jnp.where(lane < 3 * boxes, first + (lane & (boxes - 1)), -1000000)
    hot = jnp.concatenate(
        [
            jnp.where(ids == column(list_ref[n : n + 1, :]), 1.0, 0.0).astype(BF16)
            for n in range(pairs)
        ],
        axis=0,
    )
    zero = jnp.zeros((slots - 3 * boxes, lines * slots), BF16)
    source = jnp.concatenate([own_ref[...], core_ref[...], next_ref[...], zero], axis=0)
    found = dot(hot, source)
    found_ref[...] = found
    out_ref[...] = add_near(jnp.zeros(out_ref.shape, F32), found, block_ref, 0)
    fetch.wait()


def mine_kernel(
    list_ref, coef_ref, mine_ref, near_ref, found_ref, block_ref, acc_ref, total_ref
):
    boxes, slots = acc_ref.shape[1:]
    listed = own_columns(list_ref[...], boxes)
    ids = box_ids(boxes, False)
    acc = [jnp.zeros((boxes, slots), F32) for _ in range(4)]
    acc = translate(listed, ids, coef_ref, mine_ref, acc)
    for j in range(4):
        acc_ref[j] = acc[j]
    start = boxes - block_ref.shape[0]
    total_ref[...] = add_near(near_ref[...], found_ref[...], block_ref, start)


def far_kernel(
    pop_ref, list_ref, coef_ref, near_ref, acc_ref, theirs_ref, receive_ref, out_ref
):
    boxes, slots = receive_ref.shape[0], receive_ref.shape[2]
    listed = own_columns(list_ref[...], boxes)
    ids = box_ids(boxes, True)
    acc = translate(listed, ids, coef_ref, theirs_ref, [acc_ref[j] for j in range(4)])
    half = slots // 2
    low = iota((boxes, slots), 1) < half
    minus = jnp.where(low, -1.0, 1.0)
    reals, imags = [], []
    for i in range(2):
        incoming = acc[2 * i] + minus * pltpu.roll(acc[2 * i + 1], half, 1)
        reals.append(-minus * incoming)
        imags.append(pltpu.roll(incoming, half, 1))
    group = 16
    box_of_row = iota((8 * group, slots), 0) & (group - 1)
    live = live_rows(pop_ref, boxes, slots)
    for g in range(0, boxes, group):
        exact = jnp.concatenate([row[g : g + group] for row in reals + imags], axis=0)
        high = exact.astype(BF16).astype(F32)
        left_rows = jnp.concatenate([high, exact - high], axis=0)
        total = jnp.zeros(left_rows.shape, F32)
        for b in range(0, group, 2):
            left = jnp.concatenate(
                [jnp.where(box_of_row == b + h, left_rows, 0.0).astype(BF16) for h in range(2)],
                axis=1,
            )
            right = jnp.concatenate([receive_ref[g + b], receive_ref[g + b + 1]], axis=0)
            total = total + dot(left, right)
        total = total[: 4 * group] + total[4 * group :]
        for j in range(4):
            near = near_ref[j * boxes + g : j * boxes + g + group, :]
            value = total[j * group : (j + 1) * group] + near
            out_ref[j, g : g + group, :] = jnp.where(live[g : g + group], value, 0.0)


def call(kernel, out_shape, specs, out_specs, scratch=(), flops=0, size=0):
    return pl.pallas_call(
        kernel,
        out_shape=out_shape,
        in_specs=specs,
        out_specs=out_specs,
        scratch_shapes=list(scratch),
        cost_estimate=pl.CostEstimate(flops=flops, bytes_accessed=size, transcendentals=0),
        compiler_params=pltpu.CompilerParams(vmem_limit_bytes=32 * 1024 * 1024),
    )


def stay(array):
    return pltpu.with_memory_space_constraint(array, pltpu.HBM)


def body(
    currents, populations, radiate, receive, translation, far_list, far_type, near_list, near_block
):
    incs, boxes, slots = currents.shape[1:]
    lines = 2 * incs
    half = radiate.shape[3]
    far = far_list.shape[1]
    types = translation.shape[3]
    pairs = near_list.shape[1]
    wide = incs * slots
    shape = jax.ShapeDtypeStruct

    payload, pattern, masked, pop, listed, kinds, partners, trans = call(
        pattern_kernel,
        (
            shape((boxes, wide + lines * slots), BF16),
            shape((boxes, wide), BF16),
            shape((boxes, lines * slots), BF16),
            shape((1, boxes), jnp.int32),
            shape((far, 128), jnp.int32),
            shape((far, 128), jnp.int32),
            shape((pairs, boxes), jnp.int32),
            shape((2, half, types), F32),
        ),
        [HBM] * 7,
        (VMEM,) * 8,
        [
            pltpu.VMEM((lines, boxes, slots), BF16),
            pltpu.VMEM((boxes, 2 * half, slots), BF16),
            pltpu.SemaphoreType.DMA((7,)),
        ],
        flops=2 * 128 * 4096 * 128,
        size=1 << 20,
    )(
        stay(populations.reshape(1, boxes)),
        stay(currents.reshape(lines, boxes, slots)),
        stay(radiate.reshape(boxes, 2 * half, slots)),
        stay(far_list.T),
        stay(far_type.T),
        stay(near_list.T),
        stay(translation.reshape(2, half, types)),
    )

    got = {}
    for step, name in enumerate(ORDER):
        if step:
            sent = payload if name == "next" else pattern
            got[name] = lax.ppermute(sent, "box", from_line(step))
    near_core = lax.ppermute(masked, "box", from_core())

    padded = -(-types // 128) * 128
    ready = boxes // 2
    coef, pattern, block = call(
        coef_kernel,
        (
            shape((far * boxes, 2 * slots), F32),
            shape(pattern.shape, BF16),
            pltpu.VMEM((ready,) + near_block.shape[1:], BF16),
        ),
        [VMEM] * 3 + [HBM],
        (VMEM,) * 3,
        [pltpu.VMEM((2, 4 * half, padded), BF16), pltpu.SemaphoreType.DMA(())],
        flops=4 * far * boxes * padded * 2 * slots,
        size=4 << 20,
    )(kinds, trans, pattern, stay(near_block))

    around = [got[name][:, :wide] for name in ORDER[1:]]
    held = jnp.concatenate([pattern] + around, axis=0)
    planes = [lax.ppermute(held, "box", from_plane(d)) for d in PLANES]

    near, found, held, rest = call(
        near_kernel,
        (
            shape((lines * boxes, slots), F32),
            shape((pairs * boxes, lines * slots), F32),
            shape(held.shape, BF16),
            pltpu.VMEM((boxes - ready,) + near_block.shape[1:], BF16),
        ),
        [VMEM] * 6 + [HBM],
        (VMEM,) * 4,
        [pltpu.SemaphoreType.DMA(())],
        flops=2 * 64 * near_block.size,
        size=near_block.size,
    )(partners, masked, near_core, got["next"][:, wide:], held, block, stay(near_block))

    mine = jnp.concatenate([held] + planes, axis=0)
    theirs = lax.ppermute(mine, "box", from_core())
    acc, near = call(
        mine_kernel,
        (shape((lines, boxes, slots), F32), shape(near.shape, F32)),
        [VMEM] * 6,
        (VMEM, VMEM),
        flops=1024 * 1024 * 256,
        size=2 << 20,
    )(listed, coef, mine, near, found, rest)

    part = call(
        far_kernel,
        shape((lines, boxes, slots), F32),
        [VMEM] * 7,
        VMEM,
        flops=1024 * 1024 * 256,
        size=4 << 20,
    )(pop, listed, coef, near, acc, theirs, receive.reshape(boxes, 2 * half, slots))

    reps = lax.axis_size("rep")
    others = {
        d: lax.ppermute(part, "rep", [(r ^ d, r) for r in range(reps)]) for d in REPS
    }
    total = (part + others[1]) + (others[2] + others[3])
    return total.reshape(2, incs, boxes, slots)


def solution(mesh):
    return jax.shard_map(
        body,
        mesh=mesh,
        in_specs=(
            P(None, None, "box", None),
            P("box"),
            P("box", None, "rep", None, None),
            P("box", None, "rep", None, None),
            P(None, "rep", None, None),
            P(),
            P(),
            P("box", "rep"),
            P("box", "rep", None, None, None),
        ),
        out_specs=P(None, None, "box", None),
        check_vma=False,
    )
```

```python
import jax
import jax.numpy as jnp
from jax import lax
from jax.experimental import pallas as pl
from jax.experimental.pallas import tpu as pltpu
from jax.sharding import PartitionSpec as P

F32 = jnp.float32
BF16 = jnp.bfloat16
NT = (((1,), (1,)), ((), ()))
NN = (((1,), (0,)), ((), ()))
VMEM = pl.BlockSpec(memory_space=pltpu.VMEM)
HBM = pl.BlockSpec(memory_space=pltpu.HBM)
XS = ZS = 4


def iota(shape, dim):
    return lax.broadcasted_iota(jnp.int32, shape, dim)


def dot(a, b, dims=NN):
    return lax.dot_general(a, b, dims, preferred_element_type=F32)


MOVES = {
    "own": ((0, False, False), (0, False, False)),
    "next": ((-1, False, True), (1, False, True)),
    "back": ((1, False, True), (-1, False, True)),
    "across": ((2, True, False), (2, True, False)),
}
ORDER = ("own", "next", "across", "back")
LINES = tuple(tuple(MOVES[name][core] for name in ORDER) for core in range(2))
PLANES = (2, 3, 1)
REPS = (1, 3, 2)


def moved(chip, move, along_z):
    if along_z:
        return chip // ZS * ZS + (chip + move) % ZS
    return (chip + move) % (XS * ZS)


def box_perm(source):
    places = [(chip, core) for chip in range(XS * ZS) for core in range(2)]
    pairs = []
    for chip, core in places:
        from_chip, from_core = source(chip, core)
        pairs.append((from_chip * 2 + from_core, chip * 2 + core))
    return pairs


def from_line(step):
    def source(chip, core):
        move, along_z, cross = LINES[core][step]
        return moved(chip, move, along_z), 1 - core if cross else core

    return box_perm(source)


def from_plane(d):
    return box_perm(lambda chip, core: (moved(chip, d * ZS, False), core))


def from_core():
    return box_perm(lambda chip, core: (chip, 1 - core))


def column(row):
    boxes = row.shape[1]
    diagonal = iota((boxes, boxes), 0) == iota((boxes, boxes), 1)
    return jnp.sum(jnp.where(diagonal, row, 0).astype(F32), axis=1, keepdims=True).astype(jnp.int32)


def own_columns(tile, boxes):
    place = lax.axis_index("box")
    start = (place & (128 // boxes - 1)) * boxes
    moved = pltpu.roll(tile, lax.rem(128 - start, 128), 1)
    return jnp.transpose(moved.astype(F32))[:boxes].astype(jnp.int32)


def live_rows(pop_ref, boxes, slots):
    return iota((boxes, slots), 1) < column(pop_ref[...])


def pattern_kernel(
    pop_hbm, cur_hbm, rad_hbm, list_hbm, type_hbm, near_hbm, trans_hbm,
    pay_ref, pat_ref, masked_ref, pop_ref, list_ref, type_ref, near_ref, trans_ref,
    cur_ref, rad_ref, sems,
):
    lines, boxes, slots = cur_ref.shape
    place = lax.axis_index("box")
    tile = pl.multiple_of((place >> 2) * 128, 128)
    copies = [
        pltpu.make_async_copy(pop_hbm, pop_ref, sems.at[0]),
        pltpu.make_async_copy(cur_hbm, cur_ref, sems.at[1]),
        pltpu.make_async_copy(rad_hbm, rad_ref, sems.at[2]),
        pltpu.make_async_copy(list_hbm.at[:, pl.ds(tile, 128)], list_ref, sems.at[3]),
        pltpu.make_async_copy(type_hbm.at[:, pl.ds(tile, 128)], type_ref, sems.at[4]),
        pltpu.make_async_copy(near_hbm, near_ref, sems.at[5]),
        pltpu.make_async_copy(trans_hbm, trans_ref, sems.at[6]),
    ]
    for copy in copies:
        copy.start()
    copies[0].wait()
    live = live_rows(pop_ref, boxes, slots)
    copies[1].wait()
    masked = [jnp.where(live, cur_ref[j].astype(F32), 0.0) for j in range(lines)]
    for j in range(lines):
        pay_ref[:, (2 + j) * slots : (3 + j) * slots] = masked[j].astype(BF16)
        masked_ref[:, j * slots : (j + 1) * slots] = masked[j].astype(BF16)
    rows = jnp.concatenate(masked, axis=0)
    box_of_row = iota(rows.shape, 0) & (boxes - 1)
    copies[2].wait()
    total = jnp.zeros((lines * boxes, slots), F32)
    for b in range(0, boxes, 2):
        left = jnp.concatenate(
            [jnp.where(box_of_row == b + h, rows, 0.0).astype(BF16) for h in range(2)], axis=1
        )
        right = jnp.concatenate([rad_ref[b], rad_ref[b + 1]], axis=1)
        total = total + dot(left, right, NT)
    half = slots // 2
    sign = jnp.where(iota((boxes, slots), 1) < half, -1.0, 1.0)
    for i in range(2):
        real = total[i * boxes : (i + 1) * boxes]
        imag = total[(2 + i) * boxes : (3 + i) * boxes]
        out = real + sign * pltpu.roll(imag, half, 1)
        pay_ref[:, i * slots : (i + 1) * slots] = out.astype(BF16)
        pat_ref[:, i * slots : (i + 1) * slots] = out.astype(BF16)
    for copy in copies[3:]:
        copy.wait()


def coef_kernel(
    type_ref, trans_ref, pat_ref, block_hbm, coef_ref, pass_ref, block_ref, table_ref, sem
):
    fetch = pltpu.make_async_copy(block_hbm.at[pl.ds(0, block_ref.shape[0])], block_ref, sem)
    fetch.start()
    far = type_ref.shape[0]
    boxes = pat_ref.shape[0]
    half, types = trans_ref.shape[1:]
    wide = table_ref.shape[2]
    pass_ref[...] = pat_ref[...]
    table_ref[...] = jnp.zeros_like(table_ref)
    for c in range(2):
        value = trans_ref[c]
        high = value.astype(BF16)
        low = (value - high.astype(F32)).astype(BF16)
        for k in range(2):
            place = pl.ds((2 * c + k) * half, half)
            table_ref[0, place, :types] = high
            table_ref[1, place, :types] = low
    lane = iota((boxes, wide), 1)
    kinds = own_columns(type_ref[...], boxes)
    pieces = []
    for f in range(far):
        pieces.append(jnp.where(lane == kinds[:, f : f + 1], 1.0, 0.0).astype(BF16))
    hot = jnp.concatenate(pieces, axis=0)
    coef_ref[...] = dot(hot, table_ref[0], NT) + dot(hot, table_ref[1], NT)
    fetch.wait()


def box_ids(boxes, theirs):
    place = lax.axis_index("box")
    core, chip = place & 1, place >> 1
    holder = 1 - core if theirs else core
    lane = iota((1, XS * ZS * boxes), 1)
    plane = lane // (ZS * boxes)
    slot = (lane // boxes) & (ZS - 1)
    first = jnp.full(lane.shape, 0, jnp.int32)
    for step in range(ZS):
        at = []
        for move, along_z, _ in (LINES[0][step], LINES[1][step]):
            at.append((chip & ~3) + ((chip + move) & 3) if along_z else (chip + move) & 15)
        first = jnp.where(slot == step, jnp.where(holder == 0, at[0], at[1]), first)
    shift = jnp.zeros_like(lane)
    for j, d in enumerate(PLANES):
        shift = jnp.where(plane == j + 1, d * ZS, shift)
    cross = jnp.zeros_like(lane)
    for step in range(ZS):
        if LINES[0][step][2]:
            cross = jnp.where(slot == step, 1, cross)
    return ((((first + shift) & 15) * 2 + (holder ^ cross)) * boxes) + (lane & (boxes - 1))


def translate(hot_ref, side, coef_ref, source_ref, acc):
    boxes, slots = acc[0].shape
    group = 8 * boxes
    for start in range(0, hot_ref.shape[1], group):
        source = dot(hot_ref[side, start : start + group, :], source_ref[...])
        for row in range(0, group, boxes):
            at = start + row
            straight = coef_ref[at : at + boxes, :slots]
            crossed = coef_ref[at : at + boxes, slots:]
            for i in range(2):
                value = source[row : row + boxes, i * slots : (i + 1) * slots]
                acc[2 * i] = acc[2 * i] + straight * value
                acc[2 * i + 1] = acc[2 * i + 1] + crossed * value
    return acc


def add_near(total, found, block_ref, start):
    lines, pairs = 4, block_ref.shape[1]
    boxes, slots = found.shape[0] // pairs, found.shape[1] // lines
    box_of_row = iota((lines * boxes, slots), 0) & (boxes - 1)
    lefts = []
    for n in range(pairs):
        part = [
            found[n * boxes : (n + 1) * boxes, j * slots : (j + 1) * slots] for j in range(lines)
        ]
        lefts.append(jnp.concatenate(part, axis=0))
        lefts.append(jnp.concatenate([-part[2], -part[3], part[0], part[1]], axis=0))
    for b in range(block_ref.shape[0]):
        mine = box_of_row == start + b
        for n in range(pairs):
            left = jnp.concatenate(
                [jnp.where(mine, lefts[2 * n + c], 0.0).astype(BF16) for c in range(2)], axis=1
            )
            right = jnp.concatenate([block_ref[b, n, 0], block_ref[b, n, 1]], axis=1)
            total = total + dot(left, right, NT)
    return total


def near_kernel(
    list_ref, far_ref, own_ref, core_ref, next_ref, held_ref, block_ref, block_hbm,
    out_ref, found_ref, pass_ref, hot_ref, rest_ref, sem,
):
    start = block_ref.shape[0]
    fetch = pltpu.make_async_copy(block_hbm.at[pl.ds(start, rest_ref.shape[0])], rest_ref, sem)
    fetch.start()
    pairs, boxes = list_ref.shape
    slots = out_ref.shape[1]
    lines = own_ref.shape[1] // slots
    pass_ref[...] = held_ref[...]
    place = lax.axis_index("box")
    core = place & 1
    beyond = place + 2 * core - 1
    lane = iota((boxes, slots), 1)
    first = jnp.where(
        lane < boxes,
        place * boxes,
        jnp.where(lane < 2 * boxes, (place + 1 - 2 * core) * boxes, beyond * boxes),
    )
    ids = jnp.where(lane < 3 * boxes, first + (lane & (boxes - 1)), -1000000)
    hot = jnp.concatenate(
        [
            jnp.where(ids == column(list_ref[n : n + 1, :]), 1.0, 0.0).astype(BF16)
            for n in range(pairs)
        ],
        axis=0,
    )
    zero = jnp.zeros((slots - 3 * boxes, lines * slots), BF16)
    source = jnp.concatenate([own_ref[...], core_ref[...], next_ref[...], zero], axis=0)
    found = dot(hot, source)
    found_ref[...] = found
    out_ref[...] = add_near(jnp.zeros(out_ref.shape, F32), found, block_ref, 0)
    listed = own_columns(far_ref[...], boxes)
    for side in range(2):
        wanted = box_ids(boxes, side == 1)
        for f in range(far_ref.shape[0]):
            match = jnp.where(wanted == listed[:, f : f + 1], 1.0, 0.0).astype(BF16)
            hot_ref[side, f * boxes : (f + 1) * boxes, :] = match
    fetch.wait()


def mine_kernel(
    hot_ref, coef_ref, mine_ref, near_ref, found_ref, block_ref, acc_ref, total_ref
):
    boxes, slots = acc_ref.shape[1:]
    acc = [jnp.zeros((boxes, slots), F32) for _ in range(4)]
    acc = translate(hot_ref, 0, coef_ref, mine_ref, acc)
    for j in range(4):
        acc_ref[j] = acc[j]
    start = boxes - block_ref.shape[0]
    total_ref[...] = add_near(near_ref[...], found_ref[...], block_ref, start)


def far_kernel(
    pop_ref, hot_ref, coef_ref, near_ref, acc_ref, theirs_ref, receive_ref, out_ref
):
    boxes, slots = receive_ref.shape[0], receive_ref.shape[2]
    acc = translate(hot_ref, 1, coef_ref, theirs_ref, [acc_ref[j] for j in range(4)])
    half = slots // 2
    low = iota((boxes, slots), 1) < half
    minus = jnp.where(low, -1.0, 1.0)
    reals, imags = [], []
    for i in range(2):
        incoming = acc[2 * i] + minus * pltpu.roll(acc[2 * i + 1], half, 1)
        reals.append(-minus * incoming)
        imags.append(pltpu.roll(incoming, half, 1))
    group = 16
    box_of_row = iota((8 * group, slots), 0) & (group - 1)
    live = live_rows(pop_ref, boxes, slots)
    for g in range(0, boxes, group):
        exact = jnp.concatenate([row[g : g + group] for row in reals + imags], axis=0)
        high = exact.astype(BF16).astype(F32)
        left_rows = jnp.concatenate([high, exact - high], axis=0)
        total = jnp.zeros(left_rows.shape, F32)
        for b in range(0, group, 2):
            left = jnp.concatenate(
                [jnp.where(box_of_row == b + h, left_rows, 0.0).astype(BF16) for h in range(2)],
                axis=1,
            )
            right = jnp.concatenate([receive_ref[g + b], receive_ref[g + b + 1]], axis=0)
            total = total + dot(left, right)
        total = total[: 4 * group] + total[4 * group :]
        for j in range(4):
            near = near_ref[j * boxes + g : j * boxes + g + group, :]
            value = total[j * group : (j + 1) * group] + near
            out_ref[j, g : g + group, :] = jnp.where(live[g : g + group], value, 0.0)


def call(kernel, out_shape, specs, out_specs, scratch=(), flops=0, size=0):
    return pl.pallas_call(
        kernel,
        out_shape=out_shape,
        in_specs=specs,
        out_specs=out_specs,
        scratch_shapes=list(scratch),
        cost_estimate=pl.CostEstimate(flops=flops, bytes_accessed=size, transcendentals=0),
        compiler_params=pltpu.CompilerParams(vmem_limit_bytes=32 * 1024 * 1024),
    )


def stay(array):
    return pltpu.with_memory_space_constraint(array, pltpu.HBM)


def body(
    currents, populations, radiate, receive, translation, far_list, far_type, near_list, near_block
):
    incs, boxes, slots = currents.shape[1:]
    lines = 2 * incs
    half = radiate.shape[3]
    far = far_list.shape[1]
    types = translation.shape[3]
    pairs = near_list.shape[1]
    wide = incs * slots
    shape = jax.ShapeDtypeStruct

    payload, pattern, masked, pop, listed, kinds, partners, trans = call(
        pattern_kernel,
        (
            shape((boxes, wide + lines * slots), BF16),
            shape((boxes, wide), BF16),
            shape((boxes, lines * slots), BF16),
            shape((1, boxes), jnp.int32),
            shape((far, 128), jnp.int32),
            shape((far, 128), jnp.int32),
            shape((pairs, boxes), jnp.int32),
            shape((2, half, types), F32),
        ),
        [HBM] * 7,
        (VMEM,) * 8,
        [
            pltpu.VMEM((lines, boxes, slots), BF16),
            pltpu.VMEM((boxes, 2 * half, slots), BF16),
            pltpu.SemaphoreType.DMA((7,)),
        ],
        flops=2 * 128 * 4096 * 128,
        size=1 << 20,
    )(
        stay(populations.reshape(1, boxes)),
        stay(currents.reshape(lines, boxes, slots)),
        stay(radiate.reshape(boxes, 2 * half, slots)),
        stay(far_list.T),
        stay(far_type.T),
        stay(near_list.T),
        stay(translation.reshape(2, half, types)),
    )

    got = {}
    for step, name in enumerate(ORDER):
        if step:
            sent = payload if name == "next" else pattern
            got[name] = lax.ppermute(sent, "box", from_line(step))
    near_core = lax.ppermute(masked, "box", from_core())

    padded = -(-types // 128) * 128
    ready = boxes // 2
    coef, pattern, block = call(
        coef_kernel,
        (
            shape((far * boxes, 2 * slots), F32),
            shape(pattern.shape, BF16),
            pltpu.VMEM((ready,) + near_block.shape[1:], BF16),
        ),
        [VMEM] * 3 + [HBM],
        (VMEM,) * 3,
        [pltpu.VMEM((2, 4 * half, padded), BF16), pltpu.SemaphoreType.DMA(())],
        flops=4 * far * boxes * padded * 2 * slots,
        size=4 << 20,
    )(kinds, trans, pattern, stay(near_block))

    around = [got[name][:, :wide] for name in ORDER[1:]]
    held = jnp.concatenate([pattern] + around, axis=0)
    planes = [lax.ppermute(held, "box", from_plane(d)) for d in PLANES]

    near, found, held, hot, rest = call(
        near_kernel,
        (
            shape((lines * boxes, slots), F32),
            shape((pairs * boxes, lines * slots), F32),
            shape(held.shape, BF16),
            shape((2, far * boxes, XS * ZS * boxes), BF16),
            pltpu.VMEM((boxes - ready,) + near_block.shape[1:], BF16),
        ),
        [VMEM] * 7 + [HBM],
        (VMEM,) * 5,
        [pltpu.SemaphoreType.DMA(())],
        flops=2 * 64 * near_block.size,
        size=near_block.size,
    )(partners, listed, masked, near_core, got["next"][:, wide:], held, block, stay(near_block))

    mine = jnp.concatenate([held] + planes, axis=0)
    theirs = lax.ppermute(mine, "box", from_core())
    acc, near = call(
        mine_kernel,
        (shape((lines, boxes, slots), F32), shape(near.shape, F32)),
        [VMEM] * 6,
        (VMEM, VMEM),
        flops=1024 * 1024 * 256,
        size=2 << 20,
    )(hot, coef, mine, near, found, rest)

    part = call(
        far_kernel,
        shape((lines, boxes, slots), F32),
        [VMEM] * 7,
        VMEM,
        flops=1024 * 1024 * 256,
        size=4 << 20,
    )(pop, hot, coef, near, acc, theirs, receive.reshape(boxes, 2 * half, slots))

    reps = lax.axis_size("rep")
    others = {
        d: lax.ppermute(part, "rep", [(r ^ d, r) for r in range(reps)]) for d in REPS
    }
    total = (part + others[1]) + (others[2] + others[3])
    return total.reshape(2, incs, boxes, slots)


def solution(mesh):
    return jax.shard_map(
        body,
        mesh=mesh,
        in_specs=(
            P(None, None, "box", None),
            P("box"),
            P("box", None, "rep", None, None),
            P("box", None, "rep", None, None),
            P(None, "rep", None, None),
            P(),
            P(),
            P("box", "rep"),
            P("box", "rep", None, None, None),
        ),
        out_specs=P(None, None, "box", None),
        check_vma=False,
    )
```

```python
import jax
import jax.numpy as jnp
from jax import lax
from jax.experimental import pallas as pl
from jax.experimental.pallas import tpu as pltpu
from jax.sharding import PartitionSpec as P

F32 = jnp.float32
BF16 = jnp.bfloat16
NT = (((1,), (1,)), ((), ()))
NN = (((1,), (0,)), ((), ()))
VMEM = pl.BlockSpec(memory_space=pltpu.VMEM)
HBM = pl.BlockSpec(memory_space=pltpu.HBM)
XS = ZS = 4


def iota(shape, dim):
    return lax.broadcasted_iota(jnp.int32, shape, dim)


def dot(a, b, dims=NN):
    return lax.dot_general(a, b, dims, preferred_element_type=F32)


MOVES = {
    "own": ((0, False, False), (0, False, False)),
    "next": ((-1, False, True), (1, False, True)),
    "back": ((1, False, True), (-1, False, True)),
    "across": ((2, True, False), (2, True, False)),
}
ORDER = ("own", "next", "across", "back")
LINES = tuple(tuple(MOVES[name][core] for name in ORDER) for core in range(2))
PLANES = (2, 3, 1)
REPS = (1, 3, 2)


def moved(chip, move, along_z):
    if along_z:
        return chip // ZS * ZS + (chip + move) % ZS
    return (chip + move) % (XS * ZS)


def box_perm(source):
    places = [(chip, core) for chip in range(XS * ZS) for core in range(2)]
    pairs = []
    for chip, core in places:
        from_chip, from_core = source(chip, core)
        pairs.append((from_chip * 2 + from_core, chip * 2 + core))
    return pairs


def from_line(step):
    def source(chip, core):
        move, along_z, cross = LINES[core][step]
        return moved(chip, move, along_z), 1 - core if cross else core

    return box_perm(source)


def from_plane(d):
    return box_perm(lambda chip, core: (moved(chip, d * ZS, False), core))


def from_core():
    return box_perm(lambda chip, core: (chip, 1 - core))


def column(row):
    boxes = row.shape[1]
    diagonal = iota((boxes, boxes), 0) == iota((boxes, boxes), 1)
    return jnp.sum(jnp.where(diagonal, row, 0).astype(F32), axis=1, keepdims=True).astype(jnp.int32)


def own_columns(tile, boxes):
    place = lax.axis_index("box")
    start = (place & (128 // boxes - 1)) * boxes
    moved = pltpu.roll(tile, lax.rem(128 - start, 128), 1)
    return jnp.transpose(moved.astype(F32))[:boxes].astype(jnp.int32)


def live_rows(pop_ref, boxes, slots):
    return iota((boxes, slots), 1) < column(pop_ref[...])


def pattern_kernel(
    pop_hbm, cur_hbm, rad_hbm, list_hbm, type_hbm, near_hbm, trans_hbm,
    pay_ref, pat_ref, masked_ref, pop_ref, list_ref, type_ref, near_ref, trans_ref,
    cur_ref, rad_ref, sems,
):
    lines, boxes, slots = cur_ref.shape
    place = lax.axis_index("box")
    tile = pl.multiple_of((place >> 2) * 128, 128)
    copies = [
        pltpu.make_async_copy(pop_hbm, pop_ref, sems.at[0]),
        pltpu.make_async_copy(cur_hbm, cur_ref, sems.at[1]),
        pltpu.make_async_copy(rad_hbm, rad_ref, sems.at[2]),
        pltpu.make_async_copy(list_hbm.at[:, pl.ds(tile, 128)], list_ref, sems.at[3]),
        pltpu.make_async_copy(type_hbm.at[:, pl.ds(tile, 128)], type_ref, sems.at[4]),
        pltpu.make_async_copy(near_hbm, near_ref, sems.at[5]),
        pltpu.make_async_copy(trans_hbm, trans_ref, sems.at[6]),
    ]
    for copy in copies:
        copy.start()
    copies[0].wait()
    live = live_rows(pop_ref, boxes, slots)
    copies[1].wait()
    masked = [jnp.where(live, cur_ref[j].astype(F32), 0.0) for j in range(lines)]
    for j in range(lines):
        pay_ref[:, (2 + j) * slots : (3 + j) * slots] = masked[j].astype(BF16)
        masked_ref[:, j * slots : (j + 1) * slots] = masked[j].astype(BF16)
    rows = jnp.concatenate(masked, axis=0)
    box_of_row = iota(rows.shape, 0) & (boxes - 1)
    copies[2].wait()
    total = jnp.zeros((lines * boxes, slots), F32)
    for b in range(0, boxes, 2):
        left = jnp.concatenate(
            [jnp.where(box_of_row == b + h, rows, 0.0).astype(BF16) for h in range(2)], axis=1
        )
        right = jnp.concatenate([rad_ref[b], rad_ref[b + 1]], axis=1)
        total = total + dot(left, right, NT)
    half = slots // 2
    sign = jnp.where(iota((boxes, slots), 1) < half, -1.0, 1.0)
    for i in range(2):
        real = total[i * boxes : (i + 1) * boxes]
        imag = total[(2 + i) * boxes : (3 + i) * boxes]
        out = real + sign * pltpu.roll(imag, half, 1)
        pay_ref[:, i * slots : (i + 1) * slots] = out.astype(BF16)
        pat_ref[:, i * slots : (i + 1) * slots] = out.astype(BF16)
    for copy in copies[3:]:
        copy.wait()


def coef_kernel(
    type_ref, trans_ref, pat_ref, block_hbm, coef_ref, pass_ref, block_ref, table_ref, sem
):
    fetch = pltpu.make_async_copy(block_hbm.at[pl.ds(0, block_ref.shape[0])], block_ref, sem)
    fetch.start()
    far = type_ref.shape[0]
    boxes = pat_ref.shape[0]
    half, types = trans_ref.shape[1:]
    wide = table_ref.shape[2]
    pass_ref[...] = pat_ref[...]
    table_ref[...] = jnp.zeros_like(table_ref)
    for c in range(2):
        value = trans_ref[c]
        high = value.astype(BF16)
        low = (value - high.astype(F32)).astype(BF16)
        for k in range(2):
            place = pl.ds((2 * c + k) * half, half)
            table_ref[0, place, :types] = high
            table_ref[1, place, :types] = low
    lane = iota((boxes, wide), 1)
    kinds = own_columns(type_ref[...], boxes)
    pieces = []
    for f in range(far):
        pieces.append(jnp.where(lane == kinds[:, f : f + 1], 1.0, 0.0).astype(BF16))
    hot = jnp.concatenate(pieces, axis=0)
    coef_ref[...] = dot(hot, table_ref[0], NT) + dot(hot, table_ref[1], NT)
    fetch.wait()


def box_ids(boxes, theirs):
    place = lax.axis_index("box")
    core, chip = place & 1, place >> 1
    holder = 1 - core if theirs else core
    lane = iota((1, XS * ZS * boxes), 1)
    plane = lane // (ZS * boxes)
    slot = (lane // boxes) & (ZS - 1)
    first = jnp.full(lane.shape, 0, jnp.int32)
    for step in range(ZS):
        at = []
        for move, along_z, _ in (LINES[0][step], LINES[1][step]):
            at.append((chip & ~3) + ((chip + move) & 3) if along_z else (chip + move) & 15)
        first = jnp.where(slot == step, jnp.where(holder == 0, at[0], at[1]), first)
    shift = jnp.zeros_like(lane)
    for j, d in enumerate(PLANES):
        shift = jnp.where(plane == j + 1, d * ZS, shift)
    cross = jnp.zeros_like(lane)
    for step in range(ZS):
        if LINES[0][step][2]:
            cross = jnp.where(slot == step, 1, cross)
    return ((((first + shift) & 15) * 2 + (holder ^ cross)) * boxes) + (lane & (boxes - 1))


def translate(hot_ref, side, coef_ref, source_ref, acc):
    boxes, slots = acc[0].shape
    group = 8 * boxes
    for start in range(0, hot_ref.shape[1], group):
        source = dot(hot_ref[side, start : start + group, :], source_ref[...])
        for row in range(0, group, boxes):
            at = start + row
            straight = coef_ref[at : at + boxes, :slots]
            crossed = coef_ref[at : at + boxes, slots:]
            for i in range(2):
                value = source[row : row + boxes, i * slots : (i + 1) * slots]
                acc[2 * i] = acc[2 * i] + straight * value
                acc[2 * i + 1] = acc[2 * i + 1] + crossed * value
    return acc


def add_near(total, found, block_ref, start):
    lines, pairs = 4, block_ref.shape[1]
    boxes, slots = found.shape[0] // pairs, found.shape[1] // lines
    box_of_row = iota((lines * boxes, slots), 0) & (boxes - 1)
    lefts = []
    for n in range(pairs):
        part = [
            found[n * boxes : (n + 1) * boxes, j * slots : (j + 1) * slots] for j in range(lines)
        ]
        lefts.append(jnp.concatenate(part, axis=0))
        lefts.append(jnp.concatenate([-part[2], -part[3], part[0], part[1]], axis=0))
    for b in range(block_ref.shape[0]):
        mine = box_of_row == start + b
        for n in range(pairs):
            left = jnp.concatenate(
                [jnp.where(mine, lefts[2 * n + c], 0.0).astype(BF16) for c in range(2)], axis=1
            )
            right = jnp.concatenate([block_ref[b, n, 0], block_ref[b, n, 1]], axis=1)
            total = total + dot(left, right, NT)
    return total


def near_kernel(
    list_ref, far_ref, own_ref, core_ref, next_ref, held_ref, block_ref, block_hbm,
    out_ref, found_ref, pass_ref, hot_ref, rest_ref, sem,
):
    start = block_ref.shape[0]
    fetch = pltpu.make_async_copy(block_hbm.at[pl.ds(start, rest_ref.shape[0])], rest_ref, sem)
    fetch.start()
    pairs, boxes = list_ref.shape
    slots = out_ref.shape[1]
    lines = own_ref.shape[1] // slots
    pass_ref[...] = held_ref[...]
    place = lax.axis_index("box")
    core = place & 1
    beyond = place + 2 * core - 1
    lane = iota((boxes, slots), 1)
    first = jnp.where(
        lane < boxes,
        place * boxes,
        jnp.where(lane < 2 * boxes, (place + 1 - 2 * core) * boxes, beyond * boxes),
    )
    ids = jnp.where(lane < 3 * boxes, first + (lane & (boxes - 1)), -1000000)
    hot = jnp.concatenate(
        [
            jnp.where(ids == column(list_ref[n : n + 1, :]), 1.0, 0.0).astype(BF16)
            for n in range(pairs)
        ],
        axis=0,
    )
    zero = jnp.zeros((slots - 3 * boxes, lines * slots), BF16)
    source = jnp.concatenate([own_ref[...], core_ref[...], next_ref[...], zero], axis=0)
    found = dot(hot, source)
    found_ref[...] = found
    out_ref[...] = add_near(jnp.zeros(out_ref.shape, F32), found, block_ref, 0)
    listed = own_columns(far_ref[...], boxes)
    for side in range(2):
        wanted = box_ids(boxes, side == 1)
        for f in range(far_ref.shape[0]):
            match = jnp.where(wanted == listed[:, f : f + 1], 1.0, 0.0).astype(BF16)
            hot_ref[side, f * boxes : (f + 1) * boxes, :] = match
    fetch.wait()


def mine_kernel(
    hot_ref, coef_ref, mine_ref, near_ref, found_ref, block_ref, acc_ref, total_ref
):
    boxes, slots = acc_ref.shape[1:]
    acc = [jnp.zeros((boxes, slots), F32) for _ in range(4)]
    acc = translate(hot_ref, 0, coef_ref, mine_ref, acc)
    for j in range(4):
        acc_ref[j] = acc[j]
    start = boxes - block_ref.shape[0]
    total_ref[...] = add_near(near_ref[...], found_ref[...], block_ref, start)


def far_kernel(
    pop_ref, hot_ref, coef_ref, near_ref, acc_ref, theirs_ref, receive_ref, out_ref
):
    boxes, slots = receive_ref.shape[0], receive_ref.shape[2]
    acc = translate(hot_ref, 1, coef_ref, theirs_ref, [acc_ref[j] for j in range(4)])
    half = slots // 2
    low = iota((boxes, slots), 1) < half
    minus = jnp.where(low, -1.0, 1.0)
    reals, imags = [], []
    for i in range(2):
        incoming = acc[2 * i] + minus * pltpu.roll(acc[2 * i + 1], half, 1)
        reals.append(-minus * incoming)
        imags.append(pltpu.roll(incoming, half, 1))
    group = 8
    box_of_row = iota((8 * group, slots), 0) & (group - 1)
    live = live_rows(pop_ref, boxes, slots)
    for g in range(0, boxes, group):
        exact = jnp.concatenate([row[g : g + group] for row in reals + imags], axis=0)
        high = exact.astype(BF16).astype(F32)
        left_rows = jnp.concatenate([high, exact - high], axis=0)
        total = jnp.zeros(left_rows.shape, F32)
        for b in range(0, group, 2):
            left = jnp.concatenate(
                [jnp.where(box_of_row == b + h, left_rows, 0.0).astype(BF16) for h in range(2)],
                axis=1,
            )
            right = jnp.concatenate([receive_ref[g + b], receive_ref[g + b + 1]], axis=0)
            total = total + dot(left, right)
        total = total[: 4 * group] + total[4 * group :]
        for j in range(4):
            near = near_ref[j * boxes + g : j * boxes + g + group, :]
            value = total[j * group : (j + 1) * group] + near
            out_ref[j, g : g + group, :] = jnp.where(live[g : g + group], value, 0.0)


def call(kernel, out_shape, specs, out_specs, scratch=(), flops=0, size=0):
    return pl.pallas_call(
        kernel,
        out_shape=out_shape,
        in_specs=specs,
        out_specs=out_specs,
        scratch_shapes=list(scratch),
        cost_estimate=pl.CostEstimate(flops=flops, bytes_accessed=size, transcendentals=0),
        compiler_params=pltpu.CompilerParams(vmem_limit_bytes=32 * 1024 * 1024),
    )


def stay(array):
    return pltpu.with_memory_space_constraint(array, pltpu.HBM)


def body(
    currents, populations, radiate, receive, translation, far_list, far_type, near_list, near_block
):
    incs, boxes, slots = currents.shape[1:]
    lines = 2 * incs
    half = radiate.shape[3]
    far = far_list.shape[1]
    types = translation.shape[3]
    pairs = near_list.shape[1]
    wide = incs * slots
    shape = jax.ShapeDtypeStruct

    payload, pattern, masked, pop, listed, kinds, partners, trans = call(
        pattern_kernel,
        (
            shape((boxes, wide + lines * slots), BF16),
            shape((boxes, wide), BF16),
            shape((boxes, lines * slots), BF16),
            shape((1, boxes), jnp.int32),
            shape((far, 128), jnp.int32),
            shape((far, 128), jnp.int32),
            shape((pairs, boxes), jnp.int32),
            shape((2, half, types), F32),
        ),
        [HBM] * 7,
        (VMEM,) * 8,
        [
            pltpu.VMEM((lines, boxes, slots), BF16),
            pltpu.VMEM((boxes, 2 * half, slots), BF16),
            pltpu.SemaphoreType.DMA((7,)),
        ],
        flops=2 * 128 * 4096 * 128,
        size=1 << 20,
    )(
        stay(populations.reshape(1, boxes)),
        stay(currents.reshape(lines, boxes, slots)),
        stay(radiate.reshape(boxes, 2 * half, slots)),
        stay(far_list.T),
        stay(far_type.T),
        stay(near_list.T),
        stay(translation.reshape(2, half, types)),
    )

    got = {}
    for step, name in enumerate(ORDER):
        if step:
            sent = payload if name == "next" else pattern
            got[name] = lax.ppermute(sent, "box", from_line(step))
    near_core = lax.ppermute(masked, "box", from_core())

    padded = -(-types // 128) * 128
    ready = boxes // 2
    coef, pattern, block = call(
        coef_kernel,
        (
            shape((far * boxes, 2 * slots), F32),
            shape(pattern.shape, BF16),
            pltpu.VMEM((ready,) + near_block.shape[1:], BF16),
        ),
        [VMEM] * 3 + [HBM],
        (VMEM,) * 3,
        [pltpu.VMEM((2, 4 * half, padded), BF16), pltpu.SemaphoreType.DMA(())],
        flops=4 * far * boxes * padded * 2 * slots,
        size=4 << 20,
    )(kinds, trans, pattern, stay(near_block))

    around = [got[name][:, :wide] for name in ORDER[1:]]
    held = jnp.concatenate([pattern] + around, axis=0)
    planes = [lax.ppermute(held, "box", from_plane(d)) for d in PLANES]

    near, found, held, hot, rest = call(
        near_kernel,
        (
            shape((lines * boxes, slots), F32),
            shape((pairs * boxes, lines * slots), F32),
            shape(held.shape, BF16),
            shape((2, far * boxes, XS * ZS * boxes), BF16),
            pltpu.VMEM((boxes - ready,) + near_block.shape[1:], BF16),
        ),
        [VMEM] * 7 + [HBM],
        (VMEM,) * 5,
        [pltpu.SemaphoreType.DMA(())],
        flops=2 * 64 * near_block.size,
        size=near_block.size,
    )(partners, listed, masked, near_core, got["next"][:, wide:], held, block, stay(near_block))

    mine = jnp.concatenate([held] + planes, axis=0)
    theirs = lax.ppermute(mine, "box", from_core())
    acc, near = call(
        mine_kernel,
        (shape((lines, boxes, slots), F32), shape(near.shape, F32)),
        [VMEM] * 6,
        (VMEM, VMEM),
        flops=1024 * 1024 * 256,
        size=2 << 20,
    )(hot, coef, mine, near, found, rest)

    part = call(
        far_kernel,
        shape((lines, boxes, slots), F32),
        [VMEM] * 7,
        VMEM,
        flops=1024 * 1024 * 256,
        size=4 << 20,
    )(pop, hot, coef, near, acc, theirs, receive.reshape(boxes, 2 * half, slots))

    reps = lax.axis_size("rep")
    others = {
        d: lax.ppermute(part, "rep", [(r ^ d, r) for r in range(reps)]) for d in REPS
    }
    total = (part + others[1]) + (others[2] + others[3])
    return total.reshape(2, incs, boxes, slots)


def solution(mesh):
    return jax.shard_map(
        body,
        mesh=mesh,
        in_specs=(
            P(None, None, "box", None),
            P("box"),
            P("box", None, "rep", None, None),
            P("box", None, "rep", None, None),
            P(None, "rep", None, None),
            P(),
            P(),
            P("box", "rep"),
            P("box", "rep", None, None, None),
        ),
        out_specs=P(None, None, "box", None),
        check_vma=False,
    )
```

```python
import jax
import jax.numpy as jnp
from jax import lax
from jax.experimental import pallas as pl
from jax.experimental.pallas import tpu as pltpu
from jax.sharding import PartitionSpec as P

F32 = jnp.float32
BF16 = jnp.bfloat16
NT = (((1,), (1,)), ((), ()))
NN = (((1,), (0,)), ((), ()))
VMEM = pl.BlockSpec(memory_space=pltpu.VMEM)
HBM = pl.BlockSpec(memory_space=pltpu.HBM)
XS = ZS = 4


def iota(shape, dim):
    return lax.broadcasted_iota(jnp.int32, shape, dim)


def dot(a, b, dims=NN):
    return lax.dot_general(a, b, dims, preferred_element_type=F32)


MOVES = {
    "own": ((0, False, False), (0, False, False)),
    "next": ((-1, False, True), (1, False, True)),
    "back": ((1, False, True), (-1, False, True)),
    "across": ((2, True, False), (2, True, False)),
}
ORDER = ("own", "next", "across", "back")
LINES = tuple(tuple(MOVES[name][core] for name in ORDER) for core in range(2))
PLANES = (2, 3, 1)
REPS = (1, 3, 2)


def moved(chip, move, along_z):
    if along_z:
        return chip // ZS * ZS + (chip + move) % ZS
    return (chip + move) % (XS * ZS)


def box_perm(source):
    places = [(chip, core) for chip in range(XS * ZS) for core in range(2)]
    pairs = []
    for chip, core in places:
        from_chip, from_core = source(chip, core)
        pairs.append((from_chip * 2 + from_core, chip * 2 + core))
    return pairs


def from_line(step):
    def source(chip, core):
        move, along_z, cross = LINES[core][step]
        return moved(chip, move, along_z), 1 - core if cross else core

    return box_perm(source)


def from_plane(d):
    return box_perm(lambda chip, core: (moved(chip, d * ZS, False), core))


def from_core():
    return box_perm(lambda chip, core: (chip, 1 - core))


def column(row):
    boxes = row.shape[1]
    diagonal = iota((boxes, boxes), 0) == iota((boxes, boxes), 1)
    return jnp.sum(jnp.where(diagonal, row, 0).astype(F32), axis=1, keepdims=True).astype(jnp.int32)


def own_columns(tile, boxes):
    place = lax.axis_index("box")
    start = (place & (128 // boxes - 1)) * boxes
    moved = pltpu.roll(tile, lax.rem(128 - start, 128), 1)
    return jnp.transpose(moved.astype(F32))[:boxes].astype(jnp.int32)


def live_rows(pop_ref, boxes, slots):
    return iota((boxes, slots), 1) < column(pop_ref[...])


def pattern_kernel(
    pop_hbm, cur_hbm, rad_hbm, pay_ref, pat_ref, masked_ref, pop_ref, cur_ref, rad_ref, sems
):
    lines, boxes, slots = cur_ref.shape
    copies = [
        pltpu.make_async_copy(pop_hbm, pop_ref, sems.at[0]),
        pltpu.make_async_copy(cur_hbm, cur_ref, sems.at[1]),
        pltpu.make_async_copy(rad_hbm, rad_ref, sems.at[2]),
    ]
    for copy in copies:
        copy.start()
    copies[0].wait()
    live = live_rows(pop_ref, boxes, slots)
    copies[1].wait()
    masked = [jnp.where(live, cur_ref[j].astype(F32), 0.0) for j in range(lines)]
    for j in range(lines):
        pay_ref[:, (2 + j) * slots : (3 + j) * slots] = masked[j].astype(BF16)
        masked_ref[:, j * slots : (j + 1) * slots] = masked[j].astype(BF16)
    rows = jnp.concatenate(masked, axis=0)
    box_of_row = iota(rows.shape, 0) & (boxes - 1)
    copies[2].wait()
    total = jnp.zeros((lines * boxes, slots), F32)
    for b in range(0, boxes, 2):
        left = jnp.concatenate(
            [jnp.where(box_of_row == b + h, rows, 0.0).astype(BF16) for h in range(2)], axis=1
        )
        right = jnp.concatenate([rad_ref[b], rad_ref[b + 1]], axis=1)
        total = total + dot(left, right, NT)
    half = slots // 2
    sign = jnp.where(iota((boxes, slots), 1) < half, -1.0, 1.0)
    for i in range(2):
        real = total[i * boxes : (i + 1) * boxes]
        imag = total[(2 + i) * boxes : (3 + i) * boxes]
        out = real + sign * pltpu.roll(imag, half, 1)
        pay_ref[:, i * slots : (i + 1) * slots] = out.astype(BF16)
        pat_ref[:, i * slots : (i + 1) * slots] = out.astype(BF16)

def coef_kernel(
    list_hbm, type_hbm, near_hbm, trans_hbm, pat_ref, block_hbm,
    coef_ref, pass_ref, block_ref, list_ref, near_ref, type_ref, trans_ref, table_ref, sem, sems,
):
    place = lax.axis_index("box")
    tile = pl.multiple_of((place >> 2) * 128, 128)
    copies = [
        pltpu.make_async_copy(type_hbm.at[:, pl.ds(tile, 128)], type_ref, sems.at[0]),
        pltpu.make_async_copy(trans_hbm, trans_ref, sems.at[1]),
        pltpu.make_async_copy(list_hbm.at[:, pl.ds(tile, 128)], list_ref, sems.at[2]),
        pltpu.make_async_copy(near_hbm, near_ref, sems.at[3]),
    ]
    for copy in copies:
        copy.start()
    fetch = pltpu.make_async_copy(block_hbm.at[pl.ds(0, block_ref.shape[0])], block_ref, sem)
    fetch.start()
    far = type_ref.shape[0]
    boxes = pat_ref.shape[0]
    half, types = trans_ref.shape[1:]
    wide = table_ref.shape[2]
    pass_ref[...] = pat_ref[...]
    table_ref[...] = jnp.zeros_like(table_ref)
    copies[0].wait()
    copies[1].wait()
    for c in range(2):
        value = trans_ref[c]
        high = value.astype(BF16)
        low = (value - high.astype(F32)).astype(BF16)
        for k in range(2):
            at = pl.ds((2 * c + k) * half, half)
            table_ref[0, at, :types] = high
            table_ref[1, at, :types] = low
    lane = iota((boxes, wide), 1)
    kinds = own_columns(type_ref[...], boxes)
    pieces = []
    for f in range(far):
        pieces.append(jnp.where(lane == kinds[:, f : f + 1], 1.0, 0.0).astype(BF16))
    hot = jnp.concatenate(pieces, axis=0)
    coef_ref[...] = dot(hot, table_ref[0], NT) + dot(hot, table_ref[1], NT)
    copies[2].wait()
    copies[3].wait()
    fetch.wait()


def box_ids(boxes, theirs):
    place = lax.axis_index("box")
    core, chip = place & 1, place >> 1
    holder = 1 - core if theirs else core
    lane = iota((1, XS * ZS * boxes), 1)
    plane = lane // (ZS * boxes)
    slot = (lane // boxes) & (ZS - 1)
    first = jnp.full(lane.shape, 0, jnp.int32)
    for step in range(ZS):
        at = []
        for move, along_z, _ in (LINES[0][step], LINES[1][step]):
            at.append((chip & ~3) + ((chip + move) & 3) if along_z else (chip + move) & 15)
        first = jnp.where(slot == step, jnp.where(holder == 0, at[0], at[1]), first)
    shift = jnp.zeros_like(lane)
    for j, d in enumerate(PLANES):
        shift = jnp.where(plane == j + 1, d * ZS, shift)
    cross = jnp.zeros_like(lane)
    for step in range(ZS):
        if LINES[0][step][2]:
            cross = jnp.where(slot == step, 1, cross)
    return ((((first + shift) & 15) * 2 + (holder ^ cross)) * boxes) + (lane & (boxes - 1))


def translate(hot_ref, side, coef_ref, source_ref, acc):
    boxes, slots = acc[0].shape
    group = 8 * boxes
    for start in range(0, hot_ref.shape[1], group):
        source = dot(hot_ref[side, start : start + group, :], source_ref[...])
        for row in range(0, group, boxes):
            at = start + row
            straight = coef_ref[at : at + boxes, :slots]
            crossed = coef_ref[at : at + boxes, slots:]
            for i in range(2):
                value = source[row : row + boxes, i * slots : (i + 1) * slots]
                acc[2 * i] = acc[2 * i] + straight * value
                acc[2 * i + 1] = acc[2 * i + 1] + crossed * value
    return acc


def add_near(total, found, block_ref, start):
    lines, pairs = 4, block_ref.shape[1]
    boxes, slots = found.shape[0] // pairs, found.shape[1] // lines
    box_of_row = iota((lines * boxes, slots), 0) & (boxes - 1)
    lefts = []
    for n in range(pairs):
        part = [
            found[n * boxes : (n + 1) * boxes, j * slots : (j + 1) * slots] for j in range(lines)
        ]
        lefts.append(jnp.concatenate(part, axis=0))
        lefts.append(jnp.concatenate([-part[2], -part[3], part[0], part[1]], axis=0))
    for b in range(block_ref.shape[0]):
        mine = box_of_row == start + b
        for n in range(pairs):
            left = jnp.concatenate(
                [jnp.where(mine, lefts[2 * n + c], 0.0).astype(BF16) for c in range(2)], axis=1
            )
            right = jnp.concatenate([block_ref[b, n, 0], block_ref[b, n, 1]], axis=1)
            total = total + dot(left, right, NT)
    return total


def near_kernel(
    list_ref, far_ref, own_ref, core_ref, next_ref, held_ref, block_ref, block_hbm,
    out_ref, found_ref, pass_ref, hot_ref, rest_ref, sem,
):
    start = block_ref.shape[0]
    fetch = pltpu.make_async_copy(block_hbm.at[pl.ds(start, rest_ref.shape[0])], rest_ref, sem)
    fetch.start()
    pairs, boxes = list_ref.shape
    slots = out_ref.shape[1]
    lines = own_ref.shape[1] // slots
    pass_ref[...] = held_ref[...]
    place = lax.axis_index("box")
    core = place & 1
    beyond = place + 2 * core - 1
    lane = iota((boxes, slots), 1)
    first = jnp.where(
        lane < boxes,
        place * boxes,
        jnp.where(lane < 2 * boxes, (place + 1 - 2 * core) * boxes, beyond * boxes),
    )
    ids = jnp.where(lane < 3 * boxes, first + (lane & (boxes - 1)), -1000000)
    hot = jnp.concatenate(
        [
            jnp.where(ids == column(list_ref[n : n + 1, :]), 1.0, 0.0).astype(BF16)
            for n in range(pairs)
        ],
        axis=0,
    )
    zero = jnp.zeros((slots - 3 * boxes, lines * slots), BF16)
    source = jnp.concatenate([own_ref[...], core_ref[...], next_ref[...], zero], axis=0)
    found = dot(hot, source)
    found_ref[...] = found
    out_ref[...] = add_near(jnp.zeros(out_ref.shape, F32), found, block_ref, 0)
    listed = own_columns(far_ref[...], boxes)
    for side in range(2):
        wanted = box_ids(boxes, side == 1)
        for f in range(far_ref.shape[0]):
            match = jnp.where(wanted == listed[:, f : f + 1], 1.0, 0.0).astype(BF16)
            hot_ref[side, f * boxes : (f + 1) * boxes, :] = match
    fetch.wait()


def mine_kernel(
    hot_ref, coef_ref, mine_ref, near_ref, found_ref, block_ref, acc_ref, total_ref
):
    boxes, slots = acc_ref.shape[1:]
    acc = [jnp.zeros((boxes, slots), F32) for _ in range(4)]
    acc = translate(hot_ref, 0, coef_ref, mine_ref, acc)
    for j in range(4):
        acc_ref[j] = acc[j]
    start = boxes - block_ref.shape[0]
    total_ref[...] = add_near(near_ref[...], found_ref[...], block_ref, start)


def far_kernel(
    pop_ref, hot_ref, coef_ref, near_ref, acc_ref, theirs_ref, receive_ref, out_ref
):
    boxes, slots = receive_ref.shape[0], receive_ref.shape[2]
    acc = translate(hot_ref, 1, coef_ref, theirs_ref, [acc_ref[j] for j in range(4)])
    half = slots // 2
    low = iota((boxes, slots), 1) < half
    minus = jnp.where(low, -1.0, 1.0)
    reals, imags = [], []
    for i in range(2):
        incoming = acc[2 * i] + minus * pltpu.roll(acc[2 * i + 1], half, 1)
        reals.append(-minus * incoming)
        imags.append(pltpu.roll(incoming, half, 1))
    group = 8
    box_of_row = iota((8 * group, slots), 0) & (group - 1)
    live = live_rows(pop_ref, boxes, slots)
    for g in range(0, boxes, group):
        exact = jnp.concatenate([row[g : g + group] for row in reals + imags], axis=0)
        high = exact.astype(BF16).astype(F32)
        left_rows = jnp.concatenate([high, exact - high], axis=0)
        total = jnp.zeros(left_rows.shape, F32)
        for b in range(0, group, 2):
            left = jnp.concatenate(
                [jnp.where(box_of_row == b + h, left_rows, 0.0).astype(BF16) for h in range(2)],
                axis=1,
            )
            right = jnp.concatenate([receive_ref[g + b], receive_ref[g + b + 1]], axis=0)
            total = total + dot(left, right)
        total = total[: 4 * group] + total[4 * group :]
        for j in range(4):
            near = near_ref[j * boxes + g : j * boxes + g + group, :]
            value = total[j * group : (j + 1) * group] + near
            out_ref[j, g : g + group, :] = jnp.where(live[g : g + group], value, 0.0)


def call(kernel, out_shape, specs, out_specs, scratch=(), flops=0, size=0):
    return pl.pallas_call(
        kernel,
        out_shape=out_shape,
        in_specs=specs,
        out_specs=out_specs,
        scratch_shapes=list(scratch),
        cost_estimate=pl.CostEstimate(flops=flops, bytes_accessed=size, transcendentals=0),
        compiler_params=pltpu.CompilerParams(vmem_limit_bytes=32 * 1024 * 1024),
    )


def stay(array):
    return pltpu.with_memory_space_constraint(array, pltpu.HBM)


def body(
    currents, populations, radiate, receive, translation, far_list, far_type, near_list, near_block
):
    incs, boxes, slots = currents.shape[1:]
    lines = 2 * incs
    half = radiate.shape[3]
    far = far_list.shape[1]
    types = translation.shape[3]
    pairs = near_list.shape[1]
    wide = incs * slots
    shape = jax.ShapeDtypeStruct

    payload, pattern, masked, pop = call(
        pattern_kernel,
        (
            shape((boxes, wide + lines * slots), BF16),
            shape((boxes, wide), BF16),
            shape((boxes, lines * slots), BF16),
            shape((1, boxes), jnp.int32),
        ),
        [HBM] * 3,
        (VMEM,) * 4,
        [
            pltpu.VMEM((lines, boxes, slots), BF16),
            pltpu.VMEM((boxes, 2 * half, slots), BF16),
            pltpu.SemaphoreType.DMA((3,)),
        ],
        flops=2 * 128 * 4096 * 128,
        size=1 << 20,
    )(
        stay(populations.reshape(1, boxes)),
        stay(currents.reshape(lines, boxes, slots)),
        stay(radiate.reshape(boxes, 2 * half, slots)),
    )

    got = {}
    for step, name in enumerate(ORDER):
        if step:
            sent = payload if name == "next" else pattern
            got[name] = lax.ppermute(sent, "box", from_line(step))
    near_core = lax.ppermute(masked, "box", from_core())

    padded = -(-types // 128) * 128
    ready = boxes // 2
    coef, pattern, block, listed, partners = call(
        coef_kernel,
        (
            shape((far * boxes, 2 * slots), F32),
            shape(pattern.shape, BF16),
            pltpu.VMEM((ready,) + near_block.shape[1:], BF16),
            shape((far, 128), jnp.int32),
            shape((pairs, boxes), jnp.int32),
        ),
        [HBM] * 4 + [VMEM, HBM],
        (VMEM,) * 5,
        [
            pltpu.VMEM((far, 128), jnp.int32),
            pltpu.VMEM((2, half, types), F32),
            pltpu.VMEM((2, 4 * half, padded), BF16),
            pltpu.SemaphoreType.DMA(()),
            pltpu.SemaphoreType.DMA((4,)),
        ],
        flops=4 * far * boxes * padded * 2 * slots,
        size=4 << 20,
    )(
        stay(far_list.T),
        stay(far_type.T),
        stay(near_list.T),
        stay(translation.reshape(2, half, types)),
        pattern,
        stay(near_block),
    )

    around = [got[name][:, :wide] for name in ORDER[1:]]
    held = jnp.concatenate([pattern] + around, axis=0)
    planes = [lax.ppermute(held, "box", from_plane(d)) for d in PLANES]

    near, found, held, hot, rest = call(
        near_kernel,
        (
            shape((lines * boxes, slots), F32),
            shape((pairs * boxes, lines * slots), F32),
            shape(held.shape, BF16),
            shape((2, far * boxes, XS * ZS * boxes), BF16),
            pltpu.VMEM((boxes - ready,) + near_block.shape[1:], BF16),
        ),
        [VMEM] * 7 + [HBM],
        (VMEM,) * 5,
        [pltpu.SemaphoreType.DMA(())],
        flops=2 * 64 * near_block.size,
        size=near_block.size,
    )(partners, listed, masked, near_core, got["next"][:, wide:], held, block, stay(near_block))

    mine = jnp.concatenate([held] + planes, axis=0)
    theirs = lax.ppermute(mine, "box", from_core())
    acc, near = call(
        mine_kernel,
        (shape((lines, boxes, slots), F32), shape(near.shape, F32)),
        [VMEM] * 6,
        (VMEM, VMEM),
        flops=1024 * 1024 * 256,
        size=2 << 20,
    )(hot, coef, mine, near, found, rest)

    part = call(
        far_kernel,
        shape((lines, boxes, slots), F32),
        [VMEM] * 7,
        VMEM,
        flops=1024 * 1024 * 256,
        size=4 << 20,
    )(pop, hot, coef, near, acc, theirs, receive.reshape(boxes, 2 * half, slots))

    reps = lax.axis_size("rep")
    others = {
        d: lax.ppermute(part, "rep", [(r ^ d, r) for r in range(reps)]) for d in REPS
    }
    total = (part + others[1]) + (others[2] + others[3])
    return total.reshape(2, incs, boxes, slots)


def solution(mesh):
    return jax.shard_map(
        body,
        mesh=mesh,
        in_specs=(
            P(None, None, "box", None),
            P("box"),
            P("box", None, "rep", None, None),
            P("box", None, "rep", None, None),
            P(None, "rep", None, None),
            P(),
            P(),
            P("box", "rep"),
            P("box", "rep", None, None, None),
        ),
        out_specs=P(None, None, "box", None),
        check_vma=False,
    )
```

```python
import jax
import jax.numpy as jnp
from jax import lax
from jax.experimental import pallas as pl
from jax.experimental.pallas import tpu as pltpu
from jax.sharding import PartitionSpec as P

F32 = jnp.float32
BF16 = jnp.bfloat16
NT = (((1,), (1,)), ((), ()))
NN = (((1,), (0,)), ((), ()))
VMEM = pl.BlockSpec(memory_space=pltpu.VMEM)
HBM = pl.BlockSpec(memory_space=pltpu.HBM)
XS = ZS = 4


def iota(shape, dim):
    return lax.broadcasted_iota(jnp.int32, shape, dim)


def dot(a, b, dims=NN):
    return lax.dot_general(a, b, dims, preferred_element_type=F32)


MOVES = {
    "own": ((0, False, False), (0, False, False)),
    "next": ((-1, False, True), (1, False, True)),
    "back": ((1, False, True), (-1, False, True)),
    "across": ((2, True, False), (2, True, False)),
}
ORDER = ("own", "next", "across", "back")
LINES = tuple(tuple(MOVES[name][core] for name in ORDER) for core in range(2))
PLANES = (2, 3, 1)
REPS = (1, 3, 2)


def moved(chip, move, along_z):
    if along_z:
        return chip // ZS * ZS + (chip + move) % ZS
    return (chip + move) % (XS * ZS)


def box_perm(source):
    places = [(chip, core) for chip in range(XS * ZS) for core in range(2)]
    pairs = []
    for chip, core in places:
        from_chip, from_core = source(chip, core)
        pairs.append((from_chip * 2 + from_core, chip * 2 + core))
    return pairs


def from_line(step):
    def source(chip, core):
        move, along_z, cross = LINES[core][step]
        return moved(chip, move, along_z), 1 - core if cross else core

    return box_perm(source)


def from_plane(d):
    return box_perm(lambda chip, core: (moved(chip, d * ZS, False), core))


def from_core():
    return box_perm(lambda chip, core: (chip, 1 - core))


def column(row):
    boxes = row.shape[1]
    diagonal = iota((boxes, boxes), 0) == iota((boxes, boxes), 1)
    return jnp.sum(jnp.where(diagonal, row, 0).astype(F32), axis=1, keepdims=True).astype(jnp.int32)


def own_columns(tile, boxes):
    place = lax.axis_index("box")
    start = (place & (128 // boxes - 1)) * boxes
    moved = pltpu.roll(tile, lax.rem(128 - start, 128), 1)
    return jnp.transpose(moved.astype(F32))[:boxes].astype(jnp.int32)


def live_rows(pop_ref, boxes, slots):
    return iota((boxes, slots), 1) < column(pop_ref[...])


def pattern_kernel(
    pop_hbm, cur_hbm, rad_hbm, pay_ref, pat_ref, masked_ref, pop_ref, cur_ref, rad_ref, sems
):
    lines, boxes, slots = cur_ref.shape
    copies = [
        pltpu.make_async_copy(pop_hbm, pop_ref, sems.at[0]),
        pltpu.make_async_copy(cur_hbm, cur_ref, sems.at[1]),
        pltpu.make_async_copy(rad_hbm, rad_ref, sems.at[2]),
    ]
    for copy in copies:
        copy.start()
    copies[0].wait()
    live = live_rows(pop_ref, boxes, slots)
    copies[1].wait()
    masked = [jnp.where(live, cur_ref[j].astype(F32), 0.0) for j in range(lines)]
    for j in range(lines):
        pay_ref[:, (2 + j) * slots : (3 + j) * slots] = masked[j].astype(BF16)
        masked_ref[:, j * slots : (j + 1) * slots] = masked[j].astype(BF16)
    rows = jnp.concatenate(masked, axis=0)
    box_of_row = iota(rows.shape, 0) & (boxes - 1)
    copies[2].wait()
    total = jnp.zeros((lines * boxes, slots), F32)
    for b in range(0, boxes, 2):
        left = jnp.concatenate(
            [jnp.where(box_of_row == b + h, rows, 0.0).astype(BF16) for h in range(2)], axis=1
        )
        right = jnp.concatenate([rad_ref[b], rad_ref[b + 1]], axis=1)
        total = total + dot(left, right, NT)
    half = slots // 2
    sign = jnp.where(iota((boxes, slots), 1) < half, -1.0, 1.0)
    for i in range(2):
        real = total[i * boxes : (i + 1) * boxes]
        imag = total[(2 + i) * boxes : (3 + i) * boxes]
        out = real + sign * pltpu.roll(imag, half, 1)
        pay_ref[:, i * slots : (i + 1) * slots] = out.astype(BF16)
        pat_ref[:, i * slots : (i + 1) * slots] = out.astype(BF16)

def coef_kernel(
    list_hbm, type_hbm, near_hbm, trans_hbm, pat_ref, block_hbm,
    coef_ref, pass_ref, block_ref, list_ref, near_ref, type_ref, trans_ref, table_ref, sem, sems,
):
    place = lax.axis_index("box")
    tile = pl.multiple_of((place >> 2) * 128, 128)
    copies = [
        pltpu.make_async_copy(type_hbm.at[:, pl.ds(tile, 128)], type_ref, sems.at[0]),
        pltpu.make_async_copy(trans_hbm, trans_ref, sems.at[1]),
        pltpu.make_async_copy(list_hbm.at[:, pl.ds(tile, 128)], list_ref, sems.at[2]),
        pltpu.make_async_copy(near_hbm, near_ref, sems.at[3]),
    ]
    for copy in copies:
        copy.start()
    fetch = pltpu.make_async_copy(block_hbm.at[pl.ds(0, block_ref.shape[0])], block_ref, sem)
    fetch.start()
    far = type_ref.shape[0]
    boxes = pat_ref.shape[0]
    half, types = trans_ref.shape[1:]
    wide = table_ref.shape[2]
    pass_ref[...] = pat_ref[...]
    table_ref[...] = jnp.zeros_like(table_ref)
    copies[0].wait()
    copies[1].wait()
    for c in range(2):
        value = trans_ref[c]
        high = value.astype(BF16)
        low = (value - high.astype(F32)).astype(BF16)
        for k in range(2):
            at = pl.ds((2 * c + k) * half, half)
            table_ref[0, at, :types] = high
            table_ref[1, at, :types] = low
    lane = iota((boxes, wide), 1)
    kinds = own_columns(type_ref[...], boxes)
    pieces = []
    for f in range(far):
        pieces.append(jnp.where(lane == kinds[:, f : f + 1], 1.0, 0.0).astype(BF16))
    hot = jnp.concatenate(pieces, axis=0)
    coef_ref[...] = dot(hot, table_ref[0], NT) + dot(hot, table_ref[1], NT)
    copies[2].wait()
    copies[3].wait()
    fetch.wait()


def box_ids(boxes, theirs):
    place = lax.axis_index("box")
    core, chip = place & 1, place >> 1
    holder = 1 - core if theirs else core
    lane = iota((1, XS * ZS * boxes), 1)
    plane = lane // (ZS * boxes)
    slot = (lane // boxes) & (ZS - 1)
    first = jnp.full(lane.shape, 0, jnp.int32)
    for step in range(ZS):
        at = []
        for move, along_z, _ in (LINES[0][step], LINES[1][step]):
            at.append((chip & ~3) + ((chip + move) & 3) if along_z else (chip + move) & 15)
        first = jnp.where(slot == step, jnp.where(holder == 0, at[0], at[1]), first)
    shift = jnp.zeros_like(lane)
    for j, d in enumerate(PLANES):
        shift = jnp.where(plane == j + 1, d * ZS, shift)
    cross = jnp.zeros_like(lane)
    for step in range(ZS):
        if LINES[0][step][2]:
            cross = jnp.where(slot == step, 1, cross)
    return ((((first + shift) & 15) * 2 + (holder ^ cross)) * boxes) + (lane & (boxes - 1))


def translate(hot_ref, side, coef_ref, source_ref, acc):
    boxes, slots = acc[0].shape
    group = 8 * boxes
    for start in range(0, hot_ref.shape[1], group):
        source = dot(hot_ref[side, start : start + group, :], source_ref[...])
        for row in range(0, group, boxes):
            at = start + row
            straight = coef_ref[at : at + boxes, :slots]
            crossed = coef_ref[at : at + boxes, slots:]
            for i in range(2):
                value = source[row : row + boxes, i * slots : (i + 1) * slots]
                acc[2 * i] = acc[2 * i] + straight * value
                acc[2 * i + 1] = acc[2 * i + 1] + crossed * value
    return acc


def add_near(total, found, block_ref, start):
    lines, pairs = 4, block_ref.shape[1]
    boxes, slots = found.shape[0] // pairs, found.shape[1] // lines
    box_of_row = iota((lines * boxes, slots), 0) & (boxes - 1)
    lefts = []
    for n in range(pairs):
        part = [
            found[n * boxes : (n + 1) * boxes, j * slots : (j + 1) * slots] for j in range(lines)
        ]
        lefts.append(jnp.concatenate(part, axis=0))
        lefts.append(jnp.concatenate([-part[2], -part[3], part[0], part[1]], axis=0))
    for b in range(block_ref.shape[0]):
        mine = box_of_row == start + b
        for n in range(pairs):
            left = jnp.concatenate(
                [jnp.where(mine, lefts[2 * n + c], 0.0).astype(BF16) for c in range(2)], axis=1
            )
            right = jnp.concatenate([block_ref[b, n, 0], block_ref[b, n, 1]], axis=1)
            total = total + dot(left, right, NT)
    return total


def near_kernel(
    list_ref, far_ref, own_ref, core_ref, next_ref, held_ref, block_ref, block_hbm,
    out_ref, found_ref, pass_ref, hot_ref, rest_ref, sem,
):
    start = block_ref.shape[0]
    fetch = pltpu.make_async_copy(block_hbm.at[pl.ds(start, rest_ref.shape[0])], rest_ref, sem)
    fetch.start()
    pairs, boxes = list_ref.shape
    slots = out_ref.shape[1]
    lines = own_ref.shape[1] // slots
    pass_ref[...] = held_ref[...]
    place = lax.axis_index("box")
    core = place & 1
    beyond = place + 2 * core - 1
    lane = iota((boxes, slots), 1)
    first = jnp.where(
        lane < boxes,
        place * boxes,
        jnp.where(lane < 2 * boxes, (place + 1 - 2 * core) * boxes, beyond * boxes),
    )
    ids = jnp.where(lane < 3 * boxes, first + (lane & (boxes - 1)), -1000000)
    hot = jnp.concatenate(
        [
            jnp.where(ids == column(list_ref[n : n + 1, :]), 1.0, 0.0).astype(BF16)
            for n in range(pairs)
        ],
        axis=0,
    )
    zero = jnp.zeros((slots - 3 * boxes, lines * slots), BF16)
    source = jnp.concatenate([own_ref[...], core_ref[...], next_ref[...], zero], axis=0)
    found = dot(hot, source)
    found_ref[...] = found
    out_ref[...] = add_near(jnp.zeros(out_ref.shape, F32), found, block_ref, 0)
    listed = own_columns(far_ref[...], boxes)
    for side in range(2):
        wanted = box_ids(boxes, side == 1)
        for f in range(far_ref.shape[0]):
            match = jnp.where(wanted == listed[:, f : f + 1], 1.0, 0.0).astype(BF16)
            hot_ref[side, f * boxes : (f + 1) * boxes, :] = match
    fetch.wait()


def mine_kernel(
    hot_ref, coef_ref, mine_ref, near_ref, found_ref, block_ref, acc_ref, total_ref
):
    boxes, slots = acc_ref.shape[1:]
    acc = [jnp.zeros((boxes, slots), F32) for _ in range(4)]
    acc = translate(hot_ref, 0, coef_ref, mine_ref, acc)
    for j in range(4):
        acc_ref[j] = acc[j]
    start = boxes - block_ref.shape[0]
    total_ref[...] = add_near(near_ref[...], found_ref[...], block_ref, start)


def far_kernel(
    pop_ref, hot_ref, coef_ref, near_ref, acc_ref, theirs_ref, receive_ref, out_ref
):
    boxes, slots = receive_ref.shape[0], receive_ref.shape[2]
    acc = translate(hot_ref, 1, coef_ref, theirs_ref, [acc_ref[j] for j in range(4)])
    half = slots // 2
    low = iota((boxes, slots), 1) < half
    minus = jnp.where(low, -1.0, 1.0)
    reals, imags = [], []
    for i in range(2):
        incoming = acc[2 * i] + minus * pltpu.roll(acc[2 * i + 1], half, 1)
        reals.append(-minus * incoming)
        imags.append(pltpu.roll(incoming, half, 1))
    group = 8
    box_of_row = iota((8 * group, slots), 0) & (group - 1)
    live = live_rows(pop_ref, boxes, slots)
    for g in range(0, boxes, group):
        exact = jnp.concatenate([row[g : g + group] for row in reals + imags], axis=0)
        high = exact.astype(BF16).astype(F32)
        left_rows = jnp.concatenate([high, exact - high], axis=0)
        total = jnp.zeros(left_rows.shape, F32)
        for b in range(0, group, 2):
            left = jnp.concatenate(
                [jnp.where(box_of_row == b + h, left_rows, 0.0).astype(BF16) for h in range(2)],
                axis=1,
            )
            right = jnp.concatenate([receive_ref[g + b], receive_ref[g + b + 1]], axis=0)
            total = total + dot(left, right)
        total = total[: 4 * group] + total[4 * group :]
        for j in range(4):
            near = near_ref[j * boxes + g : j * boxes + g + group, :]
            value = total[j * group : (j + 1) * group] + near
            out_ref[j, g : g + group, :] = jnp.where(live[g : g + group], value, 0.0)


def call(kernel, out_shape, specs, out_specs, scratch=(), flops=0, size=0):
    return pl.pallas_call(
        kernel,
        out_shape=out_shape,
        in_specs=specs,
        out_specs=out_specs,
        scratch_shapes=list(scratch),
        cost_estimate=pl.CostEstimate(flops=flops, bytes_accessed=size, transcendentals=0),
        compiler_params=pltpu.CompilerParams(vmem_limit_bytes=32 * 1024 * 1024),
    )


def stay(array):
    return pltpu.with_memory_space_constraint(array, pltpu.HBM)


def body(
    currents, populations, radiate, receive, translation, far_list, far_type, near_list, near_block
):
    incs, boxes, slots = currents.shape[1:]
    lines = 2 * incs
    half = radiate.shape[3]
    far = far_list.shape[1]
    types = translation.shape[3]
    pairs = near_list.shape[1]
    wide = incs * slots
    shape = jax.ShapeDtypeStruct

    payload, pattern, masked, pop = call(
        pattern_kernel,
        (
            shape((boxes, wide + lines * slots), BF16),
            shape((boxes, wide), BF16),
            shape((boxes, lines * slots), BF16),
            shape((1, boxes), jnp.int32),
        ),
        [HBM] * 3,
        (VMEM,) * 4,
        [
            pltpu.VMEM((lines, boxes, slots), BF16),
            pltpu.VMEM((boxes, 2 * half, slots), BF16),
            pltpu.SemaphoreType.DMA((3,)),
        ],
        flops=2 * 128 * 4096 * 128,
        size=1 << 20,
    )(
        stay(populations.reshape(1, boxes)),
        stay(currents.reshape(lines, boxes, slots)),
        stay(radiate.reshape(boxes, 2 * half, slots)),
    )

    got = {}
    for step, name in enumerate(ORDER):
        if step:
            sent = payload if name == "next" else pattern
            got[name] = lax.ppermute(sent, "box", from_line(step))
    near_core = lax.ppermute(masked, "box", from_core())

    padded = -(-types // 128) * 128
    ready = 3 * boxes // 8
    coef, pattern, block, listed, partners = call(
        coef_kernel,
        (
            shape((far * boxes, 2 * slots), F32),
            shape(pattern.shape, BF16),
            pltpu.VMEM((ready,) + near_block.shape[1:], BF16),
            shape((far, 128), jnp.int32),
            shape((pairs, boxes), jnp.int32),
        ),
        [HBM] * 4 + [VMEM, HBM],
        (VMEM,) * 5,
        [
            pltpu.VMEM((far, 128), jnp.int32),
            pltpu.VMEM((2, half, types), F32),
            pltpu.VMEM((2, 4 * half, padded), BF16),
            pltpu.SemaphoreType.DMA(()),
            pltpu.SemaphoreType.DMA((4,)),
        ],
        flops=4 * far * boxes * padded * 2 * slots,
        size=4 << 20,
    )(
        stay(far_list.T),
        stay(far_type.T),
        stay(near_list.T),
        stay(translation.reshape(2, half, types)),
        pattern,
        stay(near_block),
    )

    around = [got[name][:, :wide] for name in ORDER[1:]]
    held = jnp.concatenate([pattern] + around, axis=0)
    planes = [lax.ppermute(held, "box", from_plane(d)) for d in PLANES]

    near, found, held, hot, rest = call(
        near_kernel,
        (
            shape((lines * boxes, slots), F32),
            shape((pairs * boxes, lines * slots), F32),
            shape(held.shape, BF16),
            shape((2, far * boxes, XS * ZS * boxes), BF16),
            pltpu.VMEM((boxes - ready,) + near_block.shape[1:], BF16),
        ),
        [VMEM] * 7 + [HBM],
        (VMEM,) * 5,
        [pltpu.SemaphoreType.DMA(())],
        flops=2 * 64 * near_block.size,
        size=near_block.size,
    )(partners, listed, masked, near_core, got["next"][:, wide:], held, block, stay(near_block))

    mine = jnp.concatenate([held] + planes, axis=0)
    theirs = lax.ppermute(mine, "box", from_core())
    acc, near = call(
        mine_kernel,
        (shape((lines, boxes, slots), F32), shape(near.shape, F32)),
        [VMEM] * 6,
        (VMEM, VMEM),
        flops=1024 * 1024 * 256,
        size=2 << 20,
    )(hot, coef, mine, near, found, rest)

    part = call(
        far_kernel,
        shape((lines, boxes, slots), F32),
        [VMEM] * 7,
        VMEM,
        flops=1024 * 1024 * 256,
        size=4 << 20,
    )(pop, hot, coef, near, acc, theirs, receive.reshape(boxes, 2 * half, slots))

    reps = lax.axis_size("rep")
    others = {
        d: lax.ppermute(part, "rep", [(r ^ d, r) for r in range(reps)]) for d in REPS
    }
    total = (part + others[1]) + (others[2] + others[3])
    return total.reshape(2, incs, boxes, slots)


def solution(mesh):
    return jax.shard_map(
        body,
        mesh=mesh,
        in_specs=(
            P(None, None, "box", None),
            P("box"),
            P("box", None, "rep", None, None),
            P("box", None, "rep", None, None),
            P(None, "rep", None, None),
            P(),
            P(),
            P("box", "rep"),
            P("box", "rep", None, None, None),
        ),
        out_specs=P(None, None, "box", None),
        check_vma=False,
    )
```
